256 devices in a mesh: row: 16 (over z_lo, y), col: 16 (over x, z_hi, core).
Axes of the slice: x: 4, y: 4, z: 8 (z_hi: 2, z_lo: 4; z = z_hi * 4 + z_lo), core: 2. Of those that a mesh axis runs over, the one named last changes fastest.
Arguments:
- b_factors: bfloat16 [3, 6144, 8192], P(None, ('row', 'col')), may hold values from -1.5 to 1.5
- occ_energy: int32 [1536], replicated, may hold values from -2048 to -256
- vir_energy: int32 [6144], P(('row', 'col')), may hold values from 128 to 8192
- pair_ids: int32 [3], replicated, may hold values from 0 to 1535
Outputs:
- gamma: float32 [3, 6144, 8192], P(None, ('row', 'col'))
- density: float32 [6144, 384], P(('row', 'col'))
The draws below stay inside these ranges and needn't reach their ends.
All inputs are finite; a program needn't handle non-finite values.
Results may differ from the reference program's by a relative error of at most 0.0021.
Values may be sent and summed in bfloat16 or wider, within the bound.
A program may use at most 128 MiB of HBM per device.

```python
import jax
import jax.numpy as jnp
from jax import lax

V = 6144
NAUX = 8192
NOCC = 1536
JPAIRS = 2
N_ROW = 16


def touch_ends(result, stream_key, low, high):
    longest = result.shape.index(max(result.shape))
    spots = []
    for shift in (0, 1):
        where = [jax.random.randint(jax.random.fold_in(stream_key, axis), (), 0, length) for axis, length in enumerate(result.shape)]
        where[longest] = (where[longest] + shift) % result.shape[longest]
        spots.append(tuple(where))
    return result.at[spots[0]].set(low).at[spots[1]].set(high)


def block_scale(rng, shape, pieces, low, top_value):
    gain = 1.0
    for position, parts in pieces:
        heights = jax.random.uniform(jax.random.fold_in(jax.random.fold_in(rng, 6), position), (parts,), jnp.float32, low / len(pieces), top_value / len(pieces))
        gain = gain * jnp.repeat(jnp.exp(heights), shape[position] // parts).reshape((-1,) + (1,) * (len(shape) - 1 - position))
    return gain


def bell_draw(key, shape, spread, most, pieces=(), held_as=jnp.bfloat16):
    result = jax.random.normal(key, shape, jnp.float32) * spread
    if len(pieces) > 0:
        result = block_scale(key, shape, pieces, -0.22, 0.18) * result
    return jnp.clip(result, min=-most, max=most).astype(held_as)


def setup_inputs(seed: int = 0) -> dict:
    splits = jax.random.split(jax.random.key(seed), 5)
    b_factors = bell_draw(splits[0], (JPAIRS + 1, V, NAUX), 0.105, 1.5, ((1, 256),))
    occ_energy = touch_ends(jax.random.randint(splits[1], (NOCC,), -2048, -255), jax.random.fold_in(splits[1], 1), -2048, (-255) - 1).astype(jnp.int32)
    vir_energy = touch_ends(jax.random.randint(splits[2], (V,), 128, 8193), jax.random.fold_in(splits[2], 1), 128, 8192).astype(jnp.int32)
    pair_ids = jax.random.randint(splits[3], (JPAIRS + 1,), 0, NOCC).astype(jnp.int32)
    return {"b_factors": b_factors, "occ_energy": occ_energy, "vir_energy": vir_energy, "pair_ids": pair_ids}


def reference(b_factors, occ_energy, vir_energy, pair_ids):
    occ = occ_energy.astype(jnp.float32) / 1024.0
    vir = vir_energy.astype(jnp.float32) / 1024.0
    first = b_factors[0]
    nrow = N_ROW
    va = V // nrow
    contract = (((1,), (1,)), ((), ()))
    shifts = [occ[pair_ids[0]] + occ[pair_ids[1 + k]] for k in range(JPAIRS)]
    seconds = [b_factors[1 + k] for k in range(JPAIRS)]
    gamma_seconds = [jnp.zeros((V, NAUX), jnp.float32) for k in range(JPAIRS)]
    gamma_rows = []
    dens_rows = []
    for block in range(nrow):
        rows = first[block * va:(block + 1) * va]
        amps = []
        for k in range(JPAIRS):
            integral = lax.dot_general(rows, seconds[k], contract, preferred_element_type=jnp.float32)
            denom = shifts[k] - vir[block * va:(block + 1) * va][:, None] - vir[None, :]
            amps.append((integral / denom).astype(jnp.bfloat16))
        total = jnp.zeros((va, NAUX), jnp.float32)
        for k in range(JPAIRS):
            total = total + jnp.dot(amps[k], seconds[k], preferred_element_type=jnp.float32)
        gamma_rows.append(total)
        dens = jnp.zeros((va, va), jnp.float32)
        for k in range(JPAIRS):
            term = lax.dot_general(amps[k], rows, (((0,), (0,)), ((), ())), preferred_element_type=jnp.float32)
            gamma_seconds[k] = gamma_seconds[k] + term
            dens = dens + lax.dot_general(amps[k], amps[k], contract, preferred_element_type=jnp.float32)
        dens_rows.append(dens)
    gamma = jnp.stack([jnp.concatenate(gamma_rows, axis=0)] + gamma_seconds)
    density = jnp.concatenate(dens_rows, axis=0)
    return gamma, density
```

```python
import jax
import jax.numpy as jnp
from jax import lax
from jax.experimental import pallas as pl
from jax.experimental.pallas import tpu as pltpu
from jax.sharding import PartitionSpec as P

MESH = pl.DeviceIdType.MESH
F32, BF16 = jnp.float32, jnp.bfloat16
NT = (((1,), (1,)), ((), ()))

R = 24
RC = 2 * R
HALF = 4096
EXT = 128
WID = HALF + EXT
CUT = 2176
Q = 2048
W0 = Q + 128
ROWS = 16 * RC
NMSG = 128


def kernel(vir_ref, occ_ref, pid_ref, b_ref, gamma_ref, dens_ref,
           A, B, st, snd, ip, ir, amp, ampt, ampd,
           acc0, hold0, l0, d0, rl0, rd0, rm0,
           acc1, hold1, l1, d1, rl1, rd1, rm1,
           rz, rp, f0, f1, ssem, rsem, osem):
    row, col = lax.axis_index("row"), lax.axis_index("col")
    x, y, z, c = col // 4, row % 4, (col // 2) % 2 * 4 + row // 4, col % 2

    def dev(x, y, z, c):
        return (z % 4 * 4 + y, x * 4 + z // 4 * 2 + c)

    xs = [dev((x + 1) % 4, y, z, c), dev((x + 3) % 4, y, z, c)]
    ys = [dev(x, (y + 1) % 4, z, c), dev(x, (y + 3) % 4, z, c)]
    zs = [dev(x, y, (z + 2) % 8, c), dev(x, y, (z + 6) % 8, c)]
    far = dev(x, y, (z + 4) % 8, c)
    pair = dev(x, y, z + 1 - 2 * (z % 2), c)
    core = dev(x, y, z, 1 - c)
    peers = xs + ys + zs + [far, pair, core]

    barrier = pltpu.get_barrier_semaphore()
    for p in peers:
        pl.semaphore_signal(barrier, inc=1, device_id=p, device_id_type=MESH)

    count = [0]

    def msg(src, dst, to):
        i = count[0]
        count[0] += 1
        return pltpu.make_async_remote_copy(
            src_ref=src, dst_ref=dst, send_sem=ssem.at[i], recv_sem=rsem.at[i],
            device_id=to, device_id_type=MESH)

    sent = []

    def go(m, later=True):
        m.start()
        if later:
            sent.append(m)
        return m

    lane = lax.broadcasted_iota(jnp.int32, (R, EXT), 1)
    e = vir_ref[...]
    diag = lax.broadcasted_iota(jnp.int32, (R, R), 0) == lax.broadcasted_iota(jnp.int32, (R, R), 1)
    e_hi = jnp.sum(jnp.where(diag, (e >> 6).astype(F32), 0.0), axis=1, keepdims=True) * (64.0 / 1024.0)
    e_lo = jnp.sum(jnp.where(diag, (e & 63).astype(F32), 0.0), axis=1, keepdims=True) * (1.0 / 1024.0)
    occ = occ_ref[...]
    place = lax.broadcasted_iota(jnp.int32, occ.shape, 0) * occ.shape[1] + lax.broadcasted_iota(
        jnp.int32, occ.shape, 1)

    def level(k):
        picked = jnp.where(place == pid_ref[k], occ.astype(F32), 0.0)
        return jnp.sum(jnp.sum(picked, axis=1, keepdims=True), axis=0, keepdims=True)

    zero = jnp.zeros((R, EXT), F32)
    exts = [jnp.where(lane == 0, e_hi, jnp.where(lane == 1, e_lo, jnp.where(
        lane < 4, 1.0, jnp.where(lane < 6, -1.0, zero))))]
    for k in range(2):
        s = level(0) + level(1 + k)
        s_hi = jnp.floor(s * (1.0 / 64.0))
        s_lo = s - s_hi * 64.0
        exts.append(jnp.where(lane < 2, 1.0, jnp.where(lane == 2, e_hi, jnp.where(lane == 3, e_lo, jnp.where(
            lane == 4, s_hi * (64.0 / 1024.0), jnp.where(lane == 5, s_lo * (1.0 / 1024.0), zero))))))

    mine = pl.multiple_of(c * R, 8)
    theirs = pl.multiple_of((1 - c) * R, 8)

    @pl.loop(0, HALF // 512)
    def _(n):
        o = n * 512
        for m in range(3):
            st[m, pl.ds(mine, R), pl.ds(pl.multiple_of(o, 128), 512)] = b_ref[
                m, :, pl.ds(pl.multiple_of(c * HALF + o, 128), 512)].astype(F32)
            snd[m, :, pl.ds(pl.multiple_of(o, 128), 512)] = b_ref[
                m, :, pl.ds(pl.multiple_of((1 - c) * HALF + o, 128), 512)].astype(F32)

    for m in range(3):
        st[m, pl.ds(mine, R), HALF:] = exts[m]
        snd[m, :, HALF:] = exts[m]

    pl.semaphore_wait(barrier, len(peers))

    swap = go(msg(snd, st.at[:, pl.ds(mine, R)], core))
    swap.wait_recv()

    @pl.loop(0, 3)
    def _(n):
        o = pl.ds(pl.multiple_of(n * 1408, 128), 1408)
        A[0:RC, o] = st[0, :, o].astype(BF16)
        for k in range(2):
            B[k * RC:(k + 1) * RC, o] = st[1 + k, :, o].astype(BF16)

    H = [pl.ds(0, CUT), pl.ds(CUT, WID - CUT)]

    class Ring:
        def __init__(self, buf, at, n, to):
            rows = lambda s: pl.ds(at[s], n)
            self.own = [[msg(buf.at[rows(0), H[h]], buf.at[rows((3, 1)[d]), H[h]], to[d]) for h in range(2)]
                        for d in range(2)]
            self.fwd = [msg(buf.at[rows((3, 1)[d]), H[d]], buf.at[rows(2), H[d]], to[d]) for d in range(2)]

        def first(self):
            for d in range(2):
                go(self.own[d][d])

        def second(self):
            for d in range(2):
                go(self.own[d][1 - d])

        def forward(self):
            for d in range(2):
                self.own[d][d].wait_recv()
                go(self.fwd[d])

        def finish(self):
            for d in range(2):
                self.own[d][1 - d].wait_recv()
            for d in range(2):
                self.fwd[d].wait_recv()

    zr = Ring(A, [i * 4 * RC for i in range(4)], RC, zs)
    xr = [Ring(A, [(i * 4 + j) * RC for j in range(4)], RC, xs) for i in range(4)]
    yr = [Ring(B, [(b * 4 + j) * 2 * RC for j in range(4)], 2 * RC, ys) for b in range(2)]
    pr = [msg(B.at[pl.ds(0, 2 * RC), H[h]], B.at[pl.ds(8 * RC, 2 * RC), H[h]], pair) for h in range(2)]

    zr.first()
    xr[0].first()
    yr[0].first()
    zr.second()
    xr[0].second()
    yr[0].second()
    go(pr[0])
    go(pr[1])
    xr[0].forward()
    zr.forward()
    go(xr[3].own[0][0])
    go(xr[1].own[1][1])
    go(xr[3].own[1][0])
    go(xr[1].own[0][1])
    yr[0].forward()
    for d in range(2):
        zr.own[d][1 - d].wait_recv()
    go(xr[3].own[0][1])
    go(xr[1].own[1][0])
    go(xr[3].own[1][1])
    go(xr[1].own[0][0])
    for h in range(2):
        pr[h].wait_recv()
    yr[1].first()
    yr[1].second()
    xr[3].forward()
    xr[1].forward()
    for d in range(2):
        zr.fwd[d].wait_recv()
    xr[2].first()
    xr[2].second()
    xr[2].forward()
    yr[1].forward()
    for r in [xr[0], yr[0], xr[3], xr[1], xr[2], yr[1]]:
        r.finish()

    HR = ROWS // 2
    parts = []
    for h in range(2):
        rows = pl.ds(h * HR, HR)

        @pl.loop(0, ROWS // 256)
        def _(n):
            o = pl.ds(pl.multiple_of(n * 256, 256), 256)
            ip[rows, o] = lax.dot_general(A[rows, 0:HALF], B[o, 0:HALF], NT, preferred_element_type=F32)

        parts.append(go(msg(ip.at[rows], ir.at[rows], core)))

    spot = [[((x + j) % 4 * 2 + (z + 2 * i) % 8 // 4) * RC for j in range(4)] for i in range(4)]
    for h in range(2):
        rows = pl.ds(h * HR, HR)
        parts[h].wait_recv()

        @pl.loop(0, ROWS // 256)
        def _(n):
            o = pl.ds(pl.multiple_of(n * 256, 256), 256)
            den = lax.dot_general(A[rows, HALF:], B[o, HALF:], NT, preferred_element_type=F32)
            t = ((ip[rows, o] + ir[rows, o]) / (0.0 - den)).astype(BF16)
            amp[rows, o] = t
            ampt[o, rows] = t.astype(F32).T.astype(BF16)
            for q in range(8):
                i, j = h * 2 + q // 4, q % 4
                to = pl.multiple_of((i % 2) * HR + spot[i][j], 16)
                ampd[pl.ds(to, RC), o] = t[q * RC:(q + 1) * RC]

    def store(b, w, cs, out, h, n, acc, hold, l, d):
        acc[b, h, :, cs] = out[0:n]
        l[b, h, :, cs] = out[2 * n:3 * n].astype(BF16)
        if h == 0:
            hold[w, 0, :, cs] = out[n:2 * n]
            d[b, 1, :, cs] = out[3 * n:4 * n].astype(BF16)
        else:
            hold[w, 1, :, cs] = out[3 * n:4 * n]
            d[b, 0, :, cs] = out[n:2 * n].astype(BF16)

    def product0(i):
        for h in range(2):
            lhs = amp[i * 4 * RC:(i + 1) * 4 * RC, :]

            @pl.loop(0, Q // 512)
            def _(n):
                o = pl.multiple_of(n * 512, 512)
                out = jnp.dot(lhs, B[:, pl.ds(o + h * Q, 512)], preferred_element_type=F32)
                store(i, 0, pl.ds(o, 512), out, h, RC, acc0, hold0, l0, d0)

            rhs = ampd[pl.ds(pl.multiple_of((i % 2) * HR + h * 128 + c * 128, 128), 128), :]
            out = lax.dot_general(lhs, rhs, NT, preferred_element_type=F32)
            store(i, 0, pl.ds(Q, 128), out, h, RC, acc0, hold0, l0, d0)

    def product1(b):
        for h in range(2):
            @pl.loop(0, Q // 256)
            def _(n):
                o = pl.multiple_of(n * 256, 256)
                out = jnp.dot(ampt[b * HR:(b + 1) * HR, :], A[:, pl.ds(o + h * Q, 256)], preferred_element_type=F32)
                store(b, b, pl.ds(o, 256), out, h, 2 * RC, acc1, hold1, l1, d1)

    class Sum:
        def __init__(self, b, w, to, acc, hold, l, d, rl, rd, rm):
            self.b, self.w, self.acc, self.hold, self.l, self.rd, self.rl, self.rm = b, w, acc, hold, l, rd, rl, rm
            self.m1 = [msg(l.at[b, f], rl.at[b, f], to[f]) for f in range(2)]
            self.md = [msg(d.at[b, f], rd.at[b, f], to[f]) for f in range(2)]
            self.m2 = [msg(l.at[b, f], rm.at[b, f], to[f]) for f in range(2)]

        def start(self):
            for m in self.m1:
                go(m, False)
            for m in self.md:
                go(m, False)

        def relay(self):
            for f in range(2):
                self.m1[f].wait_send()
                self.m1[f].wait_recv()
                self.l[self.b, f] = (self.hold[self.w, f] + self.rl[self.b, f].astype(F32)).astype(BF16)
                go(self.m2[f])

        def finish(self):
            for f in range(2):
                self.md[f].wait_send()
                self.md[f].wait_recv()
            for f in range(2):
                self.m2[f].wait_recv()
                self.acc[self.b, f] = (self.acc[self.b, f] + self.rm[self.b, f].astype(F32)
                                       + self.rd[self.b, 1 - f].astype(F32))

    s0 = [Sum(i, 0, xs, acc0, hold0, l0, d0, rl0, rd0, rm0) for i in range(4)]
    s1 = [Sum(b, b, ys, acc1, hold1, l1, d1, rl1, rd1, rm1) for b in range(2)]
    mz = [None] + [msg(d0.at[i], rz.at[3 - i], (zs[0], far, zs[1])[i - 1]) for i in (1, 2, 3)]
    mp = msg(d1.at[1], rp, pair)

    def onward0(i):
        s0[i].finish()
        d0[i] = acc0[i].astype(BF16)
        go(mz[i])

    product0(2)
    s0[2].start()
    product1(1)
    s1[1].start()
    s0[2].relay()
    product0(1)
    s0[1].start()
    product1(0)
    s1[1].relay()
    s1[0].start()
    onward0(2)
    s0[1].relay()
    product0(3)
    s0[3].start()
    onward0(1)
    s1[1].finish()
    d1[1] = acc1[1].astype(BF16)
    go(mp)
    s0[3].relay()
    product0(0)
    s0[0].start()
    s1[0].relay()
    onward0(3)
    s0[0].relay()
    s0[0].finish()
    for i in (2, 1, 3):
        mz[i].wait_recv()
    for h in range(2):
        acc0[0, h] = acc0[0, h] + rz[0, h].astype(F32) + rz[1, h].astype(F32) + rz[2, h].astype(F32)
    x0 = go(msg(acc0.at[0, :, pl.ds(theirs, R)], f0, core))
    outs = []

    def put(src, dst):
        cp = pltpu.make_async_copy(src, dst, osem.at[len(outs)])
        cp.start()
        outs.append(cp)

    def cols(core_, h):
        return pl.ds(pl.multiple_of(core_ * HALF + h * Q, 128), Q)

    for h in range(2):
        put(acc0.at[0, h, pl.ds(mine, R), pl.ds(0, Q)], gamma_ref.at[0, :, cols(c, h)])
        put(acc0.at[0, h, pl.ds(mine, R), pl.ds(Q, 128)],
            dens_ref.at[:, pl.ds(pl.multiple_of((c + h) * 128, 128), 128)])
    mp.wait_recv()
    s1[0].finish()
    for h in range(2):
        acc1[0, h] = acc1[0, h] + rp[h].astype(F32)
    x1 = []
    for k in range(2):
        x1.append(go(msg(acc1.at[0, :, pl.ds(pl.multiple_of(k * RC + theirs, 8), R)], f1.at[k], core)))
        for h in range(2):
            put(acc1.at[0, h, pl.ds(pl.multiple_of(k * RC + mine, 8), R)], gamma_ref.at[1 + k, :, cols(c, h)])
    x0.wait_recv()
    for h in range(2):
        put(f0.at[h, :, pl.ds(0, Q)], gamma_ref.at[0, :, cols(1 - c, h)])
    put(f0.at[1 - c, :, pl.ds(Q, 128)], dens_ref.at[:, pl.ds(pl.multiple_of((1 - c) * 256, 128), 128)])
    for k in range(2):
        x1[k].wait_recv()
        for h in range(2):
            put(f1.at[k, h], gamma_ref.at[1 + k, :, cols(1 - c, h)])
    for m in sent:
        m.wait_send()
    for cp in outs:
        cp.wait()


def shards(b_factors, occ_energy, vir_energy, pair_ids):
    vm = pl.BlockSpec(memory_space=pltpu.VMEM)
    V = pltpu.VMEM
    return pl.pallas_call(
        kernel,
        out_shape=(jax.ShapeDtypeStruct((3, R, 2 * HALF), F32), jax.ShapeDtypeStruct((R, 16 * R), F32)),
        in_specs=[vm, vm, pl.BlockSpec(memory_space=pltpu.SMEM), vm],
        out_specs=(pl.BlockSpec(memory_space=pl.ANY), pl.BlockSpec(memory_space=pl.ANY)),
        scratch_shapes=[
            V((ROWS, WID), BF16), V((ROWS, WID), BF16), V((3, RC, WID), F32), V((3, R, WID), F32),
            V((ROWS, ROWS), F32), V((ROWS, ROWS), F32),
            V((ROWS, ROWS), BF16), V((ROWS, ROWS), BF16), V((ROWS, ROWS), BF16),
            V((4, 2, RC, W0), F32), V((1, 2, RC, W0), F32), V((4, 2, RC, W0), BF16), V((4, 2, RC, W0), BF16),
            V((4, 2, RC, W0), BF16), V((4, 2, RC, W0), BF16), V((4, 2, RC, W0), BF16),
            V((2, 2, 2 * RC, Q), F32), V((2, 2, 2 * RC, Q), F32), V((2, 2, 2 * RC, Q), BF16),
            V((2, 2, 2 * RC, Q), BF16),
            V((2, 2, 2 * RC, Q), BF16), V((2, 2, 2 * RC, Q), BF16), V((2, 2, 2 * RC, Q), BF16),
            V((3, 2, RC, W0), BF16), V((2, 2 * RC, Q), BF16),
            V((2, R, W0), F32), V((2, 2, R, Q), F32),
            pltpu.SemaphoreType.DMA((NMSG,)), pltpu.SemaphoreType.DMA((NMSG,)), pltpu.SemaphoreType.DMA((16,)),
        ],
        compiler_params=pltpu.CompilerParams(
            collective_id=0, has_side_effects=True, vmem_limit_bytes=61 * 2**20),
        cost_estimate=pl.CostEstimate(flops=15 * 10**9, bytes_accessed=4 * 10**6, transcendentals=0),
        name="mp2",
    )(vir_energy.reshape(1, R), occ_energy.reshape(12, 128), pair_ids, b_factors)


def solution(mesh):
    in_specs = (P(None, ("row", "col"), None), P(), P(("row", "col")), P())
    out_specs = (P(None, ("row", "col"), None), P(("row", "col"), None))
    return jax.shard_map(shards, mesh=mesh, in_specs=in_specs, out_specs=out_specs, check_vma=False)
```

```python
import jax
import jax.numpy as jnp
from jax import lax
from jax.experimental import pallas as pl
from jax.experimental.pallas import tpu as pltpu
from jax.sharding import PartitionSpec as P

MESH = pl.DeviceIdType.MESH
F32, BF16 = jnp.float32, jnp.bfloat16
NT = (((1,), (1,)), ((), ()))

R = 24
RC = 2 * R
HALF = 4096
EXT = 128
WID = HALF + EXT
CUT = 2176
Q = 2048
W0 = Q // 2 + 128
ROWS = 16 * RC
NMSG = 224
Q1, Q2 = Q // 2, Q // 4
ORD = (0, 1, 3, 2)
POS = tuple(ORD.index(k) for k in range(4))
CHUNK = ((2, 2), (1, 3), (3, 1), (0, 0))


def kernel(vir_ref, occ_ref, pid_ref, b_ref, gamma_ref, dens_ref,
           A, B, st, snd, ip, ir, amp, ampt, ampd,
           acc0, hold0, l0, d0, rl0, rd0, rm0,
           acc1, hold1, l1, d1, rl1, rd1, rm1,
           rz, rp, f0, f1, ssem, rsem, osem):
    row, col = lax.axis_index("row"), lax.axis_index("col")
    x, y, z, c = col // 4, row % 4, (col // 2) % 2 * 4 + row // 4, col % 2

    def dev(x, y, z, c):
        return (z % 4 * 4 + y, x * 4 + z // 4 * 2 + c)

    xs = [dev((x + 1) % 4, y, z, c), dev((x + 3) % 4, y, z, c)]
    ys = [dev(x, (y + 1) % 4, z, c), dev(x, (y + 3) % 4, z, c)]
    zs = [dev(x, y, (z + 2) % 8, c), dev(x, y, (z + 6) % 8, c)]
    far = dev(x, y, (z + 4) % 8, c)
    pair = dev(x, y, z + 1 - 2 * (z % 2), c)
    core = dev(x, y, z, 1 - c)
    peers = xs + ys + zs + [far, pair, core]

    barrier = pltpu.get_barrier_semaphore()
    for p in peers:
        pl.semaphore_signal(barrier, inc=1, device_id=p, device_id_type=MESH)

    count = [0]

    def msg(src, dst, to):
        i = count[0]
        count[0] += 1
        return pltpu.make_async_remote_copy(
            src_ref=src, dst_ref=dst, send_sem=ssem.at[i], recv_sem=rsem.at[i],
            device_id=to, device_id_type=MESH)

    sent = []

    def go(m, later=True):
        m.start()
        if later:
            sent.append(m)
        return m

    lane = lax.broadcasted_iota(jnp.int32, (R, EXT), 1)
    e = vir_ref[...]
    diag = lax.broadcasted_iota(jnp.int32, (R, R), 0) == lax.broadcasted_iota(jnp.int32, (R, R), 1)
    e_hi = jnp.sum(jnp.where(diag, (e >> 6).astype(F32), 0.0), axis=1, keepdims=True) * (64.0 / 1024.0)
    e_lo = jnp.sum(jnp.where(diag, (e & 63).astype(F32), 0.0), axis=1, keepdims=True) * (1.0 / 1024.0)
    occ = occ_ref[...]
    place = lax.broadcasted_iota(jnp.int32, occ.shape, 0) * occ.shape[1] + lax.broadcasted_iota(
        jnp.int32, occ.shape, 1)

    def level(k):
        picked = jnp.where(place == pid_ref[k], occ.astype(F32), 0.0)
        return jnp.sum(jnp.sum(picked, axis=1, keepdims=True), axis=0, keepdims=True)

    zero = jnp.zeros((R, EXT), F32)
    exts = [jnp.where(lane == 0, e_hi, jnp.where(lane == 1, e_lo, jnp.where(
        lane < 4, 1.0, jnp.where(lane < 6, -1.0, zero))))]
    for k in range(2):
        s = level(0) + level(1 + k)
        s_hi = jnp.floor(s * (1.0 / 64.0))
        s_lo = s - s_hi * 64.0
        exts.append(jnp.where(lane < 2, 1.0, jnp.where(lane == 2, e_hi, jnp.where(lane == 3, e_lo, jnp.where(
            lane == 4, s_hi * (64.0 / 1024.0), jnp.where(lane == 5, s_lo * (1.0 / 1024.0), zero))))))

    mine = pl.multiple_of(c * R, 8)
    theirs = pl.multiple_of((1 - c) * R, 8)

    @pl.loop(0, HALF // 512)
    def _(n):
        o = n * 512
        for m in range(3):
            st[m, pl.ds(mine, R), pl.ds(pl.multiple_of(o, 128), 512)] = b_ref[
                m, :, pl.ds(pl.multiple_of(c * HALF + o, 128), 512)].astype(F32)
            snd[m, :, pl.ds(pl.multiple_of(o, 128), 512)] = b_ref[
                m, :, pl.ds(pl.multiple_of((1 - c) * HALF + o, 128), 512)].astype(F32)

    for m in range(3):
        st[m, pl.ds(mine, R), HALF:] = exts[m]
        snd[m, :, HALF:] = exts[m]

    pl.semaphore_wait(barrier, len(peers))

    swap = go(msg(snd, st.at[:, pl.ds(mine, R)], core))
    swap.wait_recv()

    @pl.loop(0, 3)
    def _(n):
        o = pl.ds(pl.multiple_of(n * 1408, 128), 1408)
        A[0:RC, o] = st[0, :, o].astype(BF16)
        for k in range(2):
            B[k * RC:(k + 1) * RC, o] = st[1 + k, :, o].astype(BF16)

    def arow(i, j):
        return (POS[i] * 4 + POS[j]) * RC

    def brow(b, j):
        return (b * 4 + POS[j]) * 2 * RC

    H = [pl.ds(0, CUT), pl.ds(CUT, WID - CUT)]
    H4 = [pl.ds(0, 1152), pl.ds(1152, 1024), pl.ds(2176, 1024), pl.ds(3200, 1024)]

    class Ring:
        def __init__(self, buf, at, n, to, cut):
            rows = lambda s: pl.ds(at[s], n)
            self.own = [[msg(buf.at[rows(0), cut[h]], buf.at[rows((3, 1)[d]), cut[h]], to[d]) for h in range(2)]
                        for d in range(2)]
            self.fwd = [msg(buf.at[rows((3, 1)[d]), cut[d]], buf.at[rows(2), cut[d]], to[d]) for d in range(2)]

        def first(self):
            for d in range(2):
                go(self.own[d][d])

        def second(self):
            for d in range(2):
                go(self.own[d][1 - d])

        def forward(self, ds=(0, 1)):
            for d in ds:
                self.own[d][d].wait_recv()
                go(self.fwd[d])

        def rest(self):
            for d in range(2):
                self.own[d][1 - d].wait_recv()

        def finish(self):
            for d in range(2):
                self.fwd[d].wait_recv()

    zown = [[msg(A.at[pl.ds(0, RC), H[h]], A.at[pl.ds(arow((3, 1)[d], 0), RC), H[h]], zs[d]) for h in range(2)]
            for d in range(2)]
    zfar = [[msg(A.at[pl.ds(arow((3, 1)[d], 0), RC), H4[2 * d + p]], A.at[pl.ds(arow(2, 0), RC), H4[2 * d + p]], zs[d])
             for p in range(2)] for d in range(2)]
    xr = [Ring(A, [arow(i, j) for j in range(4)], RC, xs, H) for i in (0, 1, 3)]
    x0, x1, x3 = xr
    x2 = [Ring(A, [arow(2, j) for j in range(4)], RC, xs, [H4[p], H4[2 + p]]) for p in range(2)]
    y0 = Ring(B, [brow(0, j) for j in range(4)], 2 * RC, ys, H)
    y1 = [Ring(B, [brow(1, j) for j in range(4)], 2 * RC, ys, [H4[p], H4[2 + p]]) for p in range(2)]
    pr = [[msg(B.at[pl.ds(0, 2 * RC), H4[p + q]], B.at[pl.ds(brow(1, 0), 2 * RC), H4[p + q]], pair) for q in (0, 2)]
          for p in range(2)]

    def integral(r, n, o0, o1, w):
        @pl.loop(0, (o1 - o0) // w)
        def _(k):
            o = pl.ds(pl.multiple_of(o0 + k * w, 128), w)
            ip[r:r + n, o] = lax.dot_general(A[r:r + n, 0:HALF], B[o, 0:HALF], NT, preferred_element_type=F32)

    def swapped(r, n, o0, o1):
        part = (pl.ds(r, n), pl.ds(o0, o1 - o0))
        return go(msg(ip.at[part], ir.at[part], core))

    def slot(s):
        i, j = ORD[s // 4], ORD[s % 4]
        return i % 2 * (ROWS // 2) + ((x + j) % 4 * 2 + (z + 2 * i) % 8 // 4) * RC

    def amplitude(r, n, o0, o1):
        @pl.loop(0, (o1 - o0) // 128)
        def _(k):
            o = pl.ds(pl.multiple_of(o0 + k * 128, 128), 128)
            rows = pl.ds(r, n)
            den = lax.dot_general(A[rows, HALF:], B[o, HALF:], NT, preferred_element_type=F32)
            t = ((ip[rows, o] + ir[rows, o]) / (0.0 - den)).astype(BF16)
            amp[rows, o] = t
            ampt[o, rows] = t.astype(F32).T.astype(BF16)
            for s in range(16):
                lo, hi = max(r, s * RC), min(r + n, s * RC + RC)
                if lo < hi:
                    ampd[pl.ds(pl.multiple_of(slot(s) + lo - s * RC, 16), hi - lo), o] = t[lo - r:hi - r]

    for d in range(2):
        go(zown[d][d])
    x0.first()
    y0.first()
    for d in range(2):
        go(zown[d][1 - d])
    x0.second()
    y0.second()
    x0.forward()
    for d in range(2):
        zown[d][d].wait_recv()
    for q in range(2):
        go(pr[0][q])
    go(x3.own[0][0])
    go(x1.own[1][1])
    go(x3.own[1][0])
    go(x1.own[0][1])
    y0.forward()
    for d in range(2):
        zown[d][1 - d].wait_recv()
    for q in range(2):
        go(pr[1][q])
    go(x3.own[0][1])
    go(x1.own[1][0])
    go(x3.own[1][1])
    go(x1.own[0][0])
    x3.forward((0,))
    x1.forward((1,))
    for q in range(2):
        pr[0][q].wait_recv()
    y1[0].first()
    y1[0].second()
    for d in range(2):
        go(zfar[d][0])
    for r in (x0, y0):
        r.rest()
        r.finish()
    integral(0, 192, 0, 384, 128)
    x3.forward((1,))
    x1.forward((0,))
    for q in range(2):
        pr[1][q].wait_recv()
    y1[1].first()
    y1[1].second()
    for d in range(2):
        go(zfar[d][1])
    for d in range(2):
        zfar[d][0].wait_recv()
    x2[0].first()
    x2[0].second()
    y1[0].forward()
    for d in range(2):
        zfar[d][1].wait_recv()
    x2[1].first()
    x2[1].second()
    x2[0].forward()
    for r in (x1, x3):
        r.rest()
        r.finish()
    integral(192, 320, 0, 384, 128)
    y1[1].forward()
    x2[1].forward()
    for r in y1:
        r.rest()
    integral(0, 512, 384, 640, 256)
    early = swapped(0, 512, 0, 640)
    early.wait_recv()
    amplitude(0, 512, 0, 640)
    for r in x2:
        r.rest()
    for r in x2 + y1:
        r.finish()
    integral(512, 256, 0, 640, 128)
    late = [swapped(512, 256, 0, 640)]
    integral(0, ROWS, 640, ROWS, 128)
    late.append(swapped(0, ROWS, 640, ROWS))
    late[0].wait_recv()
    amplitude(512, 256, 0, 640)
    late[1].wait_recv()
    amplitude(0, ROWS, 640, ROWS)

    def store(t, h, n, cs, out, acc, hold, l, d):
        acc[t, h, :, cs] = out[0:n]
        l[t, h, :, cs] = out[3 * n:4 * n].astype(BF16)
        if h == 0:
            hold[t % 2, 0, :, cs] = out[n:2 * n]
            d[t, 1, :, cs] = out[2 * n:3 * n].astype(BF16)
        else:
            hold[t % 2, 1, :, cs] = out[2 * n:3 * n]
            d[t, 0, :, cs] = out[n:2 * n].astype(BF16)

    def product0(t, h):
        i, s = CHUNK[t // 2][h], t % 2
        lhs = amp[POS[i] * 4 * RC:(POS[i] + 1) * 4 * RC, :]

        @pl.loop(0, Q1 // 512)
        def _(n):
            o = pl.multiple_of(n * 512, 512)
            out = jnp.dot(lhs, B[:, pl.ds(o + h * Q + s * Q1, 512)], preferred_element_type=F32)
            store(t, h, RC, pl.ds(o, 512), out, acc0, hold0, l0, d0)

        if s == 1:
            rhs = ampd[pl.ds(pl.multiple_of(i % 2 * (ROWS // 2) + h * 128 + c * 128, 128), 128), :]
            out = lax.dot_general(lhs, rhs, NT, preferred_element_type=F32)
            store(t, h, RC, pl.ds(Q1, 128), out, acc0, hold0, l0, d0)

    def product1(t, h):
        b, s = 1 - t // 4, t % 4
        lhs = ampt[b * ROWS // 2:(b + 1) * ROWS // 2, :]

        @pl.loop(0, Q2 // 256)
        def _(n):
            o = pl.multiple_of(n * 256, 256)
            out = jnp.dot(lhs, A[:, pl.ds(o + s * Q1 + h * Q2, 256)], preferred_element_type=F32)
            store(t, h, 2 * RC, pl.ds(o, 256), out, acc1, hold1, l1, d1)

    class Sum:
        def __init__(self, t, width, to, product, acc, hold, l, d, rl, rd, rm):
            w = pl.ds(0, width)
            full = pl.ds(0, acc.shape[2])
            self.t, self.w, self.product = t, w, product
            self.acc, self.hold, self.l, self.rd, self.rl, self.rm = acc, hold, l, rd, rl, rm
            self.m1 = [msg(l.at[t, f, full, w], rl.at[t, f, full, w], to[f]) for f in range(2)]
            self.md = [msg(d.at[t, f, full, w], rd.at[t, f, full, w], to[f]) for f in range(2)]
            self.m2 = [msg(l.at[t, f, full, w], rm.at[t, f, full, w], to[f]) for f in range(2)]

        def start(self):
            for f in range(2):
                self.product(self.t, f)
                go(self.m1[f], False)
            for f in (1, 0):
                go(self.md[f], False)

        def relay(self):
            t, w = self.t, self.w
            for f in range(2):
                self.m1[f].wait_send()
                self.m1[f].wait_recv()
                self.l[t, f, :, w] = (self.hold[t % 2, f, :, w] + self.rl[t, f, :, w].astype(F32)).astype(BF16)
                go(self.m2[f])

        def total(self, h):
            t, w = self.t, self.w
            return (self.acc[t, h, :, w] + self.rm[t, h, :, w].astype(F32) + self.rd[t, 1 - h, :, w].astype(F32))

        def finish(self):
            for f in range(2):
                self.md[f].wait_send()
                self.md[f].wait_recv()
            for f in range(2):
                self.m2[f].wait_recv()

    s0 = [Sum(t, Q1 + t % 2 * 128, xs, product0, acc0, hold0, l0, d0, rl0, rd0, rm0) for t in range(8)]
    s1 = [Sum(t, Q2, ys, product1, acc1, hold1, l1, d1, rl1, rd1, rm1) for t in range(8)]

    def zmsgs(t, k, flip):
        w = (pl.ds(0, RC), s0[t].w)
        return [msg(d0.at[(t, 1 - f if flip else f) + w], rz.at[(k, t % 2, f) + w], zs[f]) for f in range(2)]

    zl = [zmsgs(t, 0, False) for t in (0, 1)]
    zm = [zmsgs(t, 1, False) for t in (2, 3)]
    zd = [zmsgs(t, 2, True) for t in (4, 5)]
    mp = [msg(d1.at[t], rp.at[t], pair) for t in range(4)]
    outs = []

    def put(src, dst):
        cp = pltpu.make_async_copy(src, dst, osem.at[len(outs)])
        cp.start()
        outs.append(cp)

    def cols(core_, o, n):
        return pl.ds(pl.multiple_of(core_ * HALF + o, 128), n)

    f0m, f1m = [], []

    def done0(t):
        s0[t].finish()
        p, s, w = t // 2, t % 2, s0[t].w
        for f in range(2):
            if p == 0:
                d0[t, f, :, w] = s0[t].total(f).astype(BF16)
                go(zl[s][f])
            elif p == 1:
                zl[s][f].wait_recv()
                d0[t, f, :, w] = (s0[t].total(f) + rz[0, s, f, :, w].astype(F32)).astype(BF16)
                go(zm[s][f])
            elif p == 2:
                d0[t, 1 - f, :, w] = s0[t].total(1 - f).astype(BF16)
                go(zd[s][f])
            else:
                zm[s][f].wait_recv()
                zd[s][f].wait_recv()
        if p == 3:
            for h in range(2):
                acc0[t, h, :, w] = (s0[t].total(h) + rz[1, s, h, :, w].astype(F32)
                                    + rz[2, s, 1 - h, :, w].astype(F32))
            f0m.append(go(msg(acc0.at[t, :, pl.ds(theirs, R), w], f0.at[s, :, :, w], core)))
            for h in range(2):
                put(acc0.at[t, h, pl.ds(mine, R), pl.ds(0, Q1)], gamma_ref.at[0, :, cols(c, h * Q + s * Q1, Q1)])
                if s == 1:
                    put(acc0.at[t, h, pl.ds(mine, R), pl.ds(Q1, 128)],
                        dens_ref.at[:, pl.ds(pl.multiple_of((c + h) * 128, 128), 128)])

    def land0(s):
        f0m[s].wait_recv()
        for h in range(2):
            put(f0.at[s, h, :, pl.ds(0, Q1)], gamma_ref.at[0, :, cols(1 - c, h * Q + s * Q1, Q1)])
        if s == 1:
            put(f0.at[s, 1 - c, :, pl.ds(Q1, 128)],
                dens_ref.at[:, pl.ds(pl.multiple_of((1 - c) * 256, 128), 128)])

    def done1(t):
        s1[t].finish()
        if t < 4:
            for h in range(2):
                d1[t, h] = s1[t].total(h).astype(BF16)
            go(mp[t])
            return
        s = t - 4
        mp[s].wait_recv()
        for h in range(2):
            acc1[t, h] = s1[t].total(h) + rp[s, h].astype(F32)
        for k in range(2):
            f1m.append(go(msg(acc1.at[t, :, pl.ds(pl.multiple_of(k * RC + theirs, 8), R)], f1.at[s, k], core)))
        for k in range(2):
            for h in range(2):
                put(acc1.at[t, h, pl.ds(pl.multiple_of(k * RC + mine, 8), R)],
                    gamma_ref.at[1 + k, :, cols(c, s * Q1 + h * Q2, Q2)])

    def land1(s):
        for k in range(2):
            f1m[s * 2 + k].wait_recv()
            for h in range(2):
                put(f1.at[s, k, h], gamma_ref.at[1 + k, :, cols(1 - c, s * Q1 + h * Q2, Q2)])

    s0[0].start()
    s1[0].start()
    s0[0].relay()
    s0[1].start()
    s1[0].relay()
    s1[1].start()
    done0(0)
    done1(0)
    for t in range(1, 8):
        if t < 7:
            s0[t + 1].start()
            s1[t + 1].start()
        s0[t].relay()
        s1[t].relay()
        if t > 1:
            done0(t - 1)
            done1(t - 1)
        if t - 2 >= 4:
            land1(t - 6)
    land0(0)
    land1(2)
    done0(7)
    done1(7)
    land0(1)
    land1(3)
    for m in sent:
        m.wait_send()
    for cp in outs:
        cp.wait()


def shards(b_factors, occ_energy, vir_energy, pair_ids):
    vm = pl.BlockSpec(memory_space=pltpu.VMEM)
    V = pltpu.VMEM
    return pl.pallas_call(
        kernel,
        out_shape=(jax.ShapeDtypeStruct((3, R, 2 * HALF), F32), jax.ShapeDtypeStruct((R, 16 * R), F32)),
        in_specs=[vm, vm, pl.BlockSpec(memory_space=pltpu.SMEM), vm],
        out_specs=(pl.BlockSpec(memory_space=pl.ANY), pl.BlockSpec(memory_space=pl.ANY)),
        scratch_shapes=[
            V((ROWS, WID), BF16), V((ROWS, WID), BF16), V((3, RC, WID), F32), V((3, R, WID), F32),
            V((ROWS, ROWS), F32), V((ROWS, ROWS), F32),
            V((ROWS, ROWS), BF16), V((ROWS, ROWS), BF16), V((ROWS, ROWS), BF16),
            V((8, 2, RC, W0), F32), V((2, 2, RC, W0), F32), V((8, 2, RC, W0), BF16), V((8, 2, RC, W0), BF16),
            V((8, 2, RC, W0), BF16), V((8, 2, RC, W0), BF16), V((8, 2, RC, W0), BF16),
            V((8, 2, 2 * RC, Q2), F32), V((2, 2, 2 * RC, Q2), F32), V((8, 2, 2 * RC, Q2), BF16),
            V((8, 2, 2 * RC, Q2), BF16),
            V((8, 2, 2 * RC, Q2), BF16), V((8, 2, 2 * RC, Q2), BF16), V((8, 2, 2 * RC, Q2), BF16),
            V((3, 2, 2, RC, W0), BF16), V((4, 2, 2 * RC, Q2), BF16),
            V((2, 2, R, W0), F32), V((4, 2, 2, R, Q2), F32),
            pltpu.SemaphoreType.DMA((NMSG,)), pltpu.SemaphoreType.DMA((NMSG,)), pltpu.SemaphoreType.DMA((64,)),
        ],
        compiler_params=pltpu.CompilerParams(
            collective_id=0, has_side_effects=True, vmem_limit_bytes=61 * 2**20),
        cost_estimate=pl.CostEstimate(flops=15 * 10**9, bytes_accessed=4 * 10**6, transcendentals=0),
        name="mp2",
    )(vir_energy.reshape(1, R), occ_energy.reshape(12, 128), pair_ids, b_factors)


def solution(mesh):
    in_specs = (P(None, ("row", "col"), None), P(), P(("row", "col")), P())
    out_specs = (P(None, ("row", "col"), None), P(("row", "col"), None))
    return jax.shard_map(shards, mesh=mesh, in_specs=in_specs, out_specs=out_specs, check_vma=False)
```

```python
import jax
import jax.numpy as jnp
from jax import lax
from jax.experimental import pallas as pl
from jax.experimental.pallas import tpu as pltpu
from jax.sharding import PartitionSpec as P

MESH = pl.DeviceIdType.MESH
F32, BF16 = jnp.float32, jnp.bfloat16
NT = (((1,), (1,)), ((), ()))

R = 24
RC = 2 * R
HALF = 4096
EXT = 128
WID = HALF + EXT
CUT = 2048
Q = 2048
W0 = Q // 2 + 128
ROWS = 16 * RC
NMSG = 224
Q1, Q2 = Q // 2, Q // 4
ORD = (0, 1, 3, 2)
POS = tuple(ORD.index(k) for k in range(4))
CHUNK = ((2, 2), (1, 3), (3, 1), (0, 0))


def kernel(vir_ref, occ_ref, pid_ref, b_hbm, gamma_ref, dens_ref,
           b_ref, A, B, st, snd, ip, ir, amp, ampt, ampd,
           acc0, hold0, l0, d0, rl0, rd0, rm0,
           acc1, hold1, l1, d1, rl1, rd1, rm1,
           rz, rp, f0, f1, ssem, rsem, osem):
    row, col = lax.axis_index("row"), lax.axis_index("col")
    x, y, z, c = col // 4, row % 4, (col // 2) % 2 * 4 + row // 4, col % 2

    def dev(x, y, z, c):
        return (z % 4 * 4 + y, x * 4 + z // 4 * 2 + c)

    xs = [dev((x + 1) % 4, y, z, c), dev((x + 3) % 4, y, z, c)]
    ys = [dev(x, (y + 1) % 4, z, c), dev(x, (y + 3) % 4, z, c)]
    zs = [dev(x, y, (z + 2) % 8, c), dev(x, y, (z + 6) % 8, c)]
    far = dev(x, y, (z + 4) % 8, c)
    pair = dev(x, y, z + 1 - 2 * (z % 2), c)
    core = dev(x, y, z, 1 - c)
    peers = xs + ys + zs + [far, pair, core]

    barrier = pltpu.get_barrier_semaphore()
    for p in peers:
        pl.semaphore_signal(barrier, inc=1, device_id=p, device_id_type=MESH)

    load = pltpu.make_async_copy(b_hbm, b_ref, osem.at[63])
    load.start()

    count = [0]

    def msg(src, dst, to):
        i = count[0]
        count[0] += 1
        return pltpu.make_async_remote_copy(
            src_ref=src, dst_ref=dst, send_sem=ssem.at[i], recv_sem=rsem.at[i],
            device_id=to, device_id_type=MESH)

    sent = []

    def go(m, later=True):
        m.start()
        if later:
            sent.append(m)
        return m

    lane = lax.broadcasted_iota(jnp.int32, (R, EXT), 1)
    e = vir_ref[...]
    diag = lax.broadcasted_iota(jnp.int32, (R, R), 0) == lax.broadcasted_iota(jnp.int32, (R, R), 1)
    e_hi = jnp.sum(jnp.where(diag, (e >> 6).astype(F32), 0.0), axis=1, keepdims=True) * (64.0 / 1024.0)
    e_lo = jnp.sum(jnp.where(diag, (e & 63).astype(F32), 0.0), axis=1, keepdims=True) * (1.0 / 1024.0)
    occ = occ_ref[...]
    place = lax.broadcasted_iota(jnp.int32, occ.shape, 0) * occ.shape[1] + lax.broadcasted_iota(
        jnp.int32, occ.shape, 1)

    def level(k):
        picked = jnp.where(place == pid_ref[k], occ.astype(F32), 0.0)
        return jnp.sum(jnp.sum(picked, axis=1, keepdims=True), axis=0, keepdims=True)

    zero = jnp.zeros((R, EXT), F32)
    exts = [jnp.where(lane == 0, e_hi, jnp.where(lane == 1, e_lo, jnp.where(
        lane < 4, 1.0, jnp.where(lane < 6, -1.0, zero))))]
    for k in range(2):
        s = level(0) + level(1 + k)
        s_hi = jnp.floor(s * (1.0 / 64.0))
        s_lo = s - s_hi * 64.0
        exts.append(jnp.where(lane < 2, 1.0, jnp.where(lane == 2, e_hi, jnp.where(lane == 3, e_lo, jnp.where(
            lane == 4, s_hi * (64.0 / 1024.0), jnp.where(lane == 5, s_lo * (1.0 / 1024.0), zero))))))

    mine = pl.multiple_of(c * R, 8)
    theirs = pl.multiple_of((1 - c) * R, 8)

    load.wait()

    @pl.loop(0, 3)
    def _(m):
        @pl.loop(0, HALF // 512)
        def _(n):
            o = pl.multiple_of(n * 512, 128)
            st[m, pl.ds(mine, R), pl.ds(o, 512)] = b_ref[m, :, pl.ds(pl.multiple_of(c * HALF + o, 128), 512)].astype(F32)
            snd[m, :, pl.ds(o, 512)] = b_ref[m, :, pl.ds(pl.multiple_of((1 - c) * HALF + o, 128), 512)].astype(F32)

    for m in range(3):
        st[m, pl.ds(mine, R), HALF:] = exts[m]
        snd[m, :, HALF:] = exts[m]

    pl.semaphore_wait(barrier, len(peers))
    swap = [go(msg(snd.at[m], st.at[m, pl.ds(mine, R)], core)) for m in range(3)]

    def arow(i, j):
        return (POS[i] * 4 + POS[j]) * RC

    def brow(b, j):
        return (b * 4 + POS[j]) * 2 * RC

    H = [pl.ds(0, CUT), pl.ds(CUT, WID - CUT)]
    H4 = [pl.ds(0, 1024), pl.ds(1024, 1024), pl.ds(2048, 1024), pl.ds(3072, WID - 3072)]

    class Ring:
        def __init__(self, buf, at, n, to, cut):
            rows = lambda s: pl.ds(at[s], n)
            self.own = [[msg(buf.at[rows(0), cut[h]], buf.at[rows((3, 1)[d]), cut[h]], to[d]) for h in range(2)]
                        for d in range(2)]
            self.fwd = [msg(buf.at[rows((3, 1)[d]), cut[d]], buf.at[rows(2), cut[d]], to[d]) for d in range(2)]

        def first(self):
            for d in range(2):
                go(self.own[d][d])

        def second(self):
            for d in range(2):
                go(self.own[d][1 - d])

        def forward(self, ds=(0, 1)):
            for d in ds:
                self.own[d][d].wait_recv()
                go(self.fwd[d])

        def rest(self):
            for d in range(2):
                self.own[d][1 - d].wait_recv()

        def finish(self):
            for d in range(2):
                self.fwd[d].wait_recv()

    zown = [[msg(A.at[pl.ds(0, RC), H[h]], A.at[pl.ds(arow((3, 1)[d], 0), RC), H[h]], zs[d]) for h in range(2)]
            for d in range(2)]
    zfar = [[msg(A.at[pl.ds(arow((3, 1)[d], 0), RC), H4[2 * d + p]], A.at[pl.ds(arow(2, 0), RC), H4[2 * d + p]], zs[d])
             for p in range(2)] for d in range(2)]
    xr = [Ring(A, [arow(i, j) for j in range(4)], RC, xs, H) for i in (0, 1, 3)]
    x0, x1, x3 = xr
    x2 = [Ring(A, [arow(2, j) for j in range(4)], RC, xs, [H4[p], H4[2 + p]]) for p in range(2)]
    y0 = Ring(B, [brow(0, j) for j in range(4)], 2 * RC, ys, H)
    y1 = [Ring(B, [brow(1, j) for j in range(4)], 2 * RC, ys, [H4[p], H4[2 + p]]) for p in range(2)]
    pr = [[msg(B.at[pl.ds(0, 2 * RC), H4[p + q]], B.at[pl.ds(brow(1, 0), 2 * RC), H4[p + q]], pair) for q in (0, 2)]
          for p in range(2)]

    def integral(r, n, o0, o1, w):
        @pl.loop(0, (o1 - o0) // w)
        def _(k):
            o = pl.ds(pl.multiple_of(o0 + k * w, 128), w)
            ip[r:r + n, o] = lax.dot_general(A[r:r + n, 0:HALF], B[o, 0:HALF], NT, preferred_element_type=F32)

    def swapped(r, n, o0, o1):
        part = (pl.ds(r, n), pl.ds(o0, o1 - o0))
        return go(msg(ip.at[part], ir.at[part], core))

    def slot(s):
        i, j = ORD[s // 4], ORD[s % 4]
        return i % 2 * (ROWS // 2) + ((x + j) % 4 * 2 + (z + 2 * i) % 8 // 4) * RC

    def amplitude(r, n, o0, o1):
        @pl.loop(0, (o1 - o0) // 128)
        def _(k):
            o = pl.ds(pl.multiple_of(o0 + k * 128, 128), 128)
            rows = pl.ds(r, n)
            den = lax.dot_general(A[rows, HALF:], B[o, HALF:], NT, preferred_element_type=F32)
            t = ((ip[rows, o] + ir[rows, o]) / (0.0 - den)).astype(BF16)
            amp[rows, o] = t
            ampt[o, rows] = t.astype(F32).T.astype(BF16)
            for s in range(16):
                lo, hi = max(r, s * RC), min(r + n, s * RC + RC)
                if lo < hi:
                    ampd[pl.ds(pl.multiple_of(slot(s) + lo - s * RC, 16), hi - lo), o] = t[lo - r:hi - r]

    def settle(buf, to, m):
        swap[m].wait_recv()

        @pl.loop(0, 3)
        def _(n):
            o = pl.ds(pl.multiple_of(n * 1408, 128), 1408)
            buf[to:to + RC, o] = st[m, :, o].astype(BF16)

    settle(A, 0, 0)
    for d in range(2):
        go(zown[d][d])
    x0.first()
    for d in range(2):
        go(zown[d][1 - d])
    x0.second()
    for k in range(2):
        settle(B, k * RC, 1 + k)
    y0.first()
    y0.second()
    x0.forward()
    for d in range(2):
        zown[d][d].wait_recv()
    for q in range(2):
        go(pr[0][q])
    go(x3.own[0][0])
    go(x1.own[1][1])
    go(x3.own[1][0])
    go(x1.own[0][1])
    y0.forward()
    for d in range(2):
        zown[d][1 - d].wait_recv()
    for q in range(2):
        go(pr[1][q])
    go(x3.own[0][1])
    go(x1.own[1][0])
    go(x3.own[1][1])
    go(x1.own[0][0])
    x3.forward((0,))
    x1.forward((1,))
    for q in range(2):
        pr[0][q].wait_recv()
    y1[0].first()
    y1[0].second()
    for d in range(2):
        go(zfar[d][0])
    for r in (x0, y0):
        r.rest()
        r.finish()
    integral(0, 192, 0, 384, 128)
    x3.forward((1,))
    x1.forward((0,))
    for q in range(2):
        pr[1][q].wait_recv()
    y1[1].first()
    y1[1].second()
    for d in range(2):
        go(zfar[d][1])
    for d in range(2):
        zfar[d][0].wait_recv()
    x2[0].first()
    x2[0].second()
    y1[0].forward()
    for d in range(2):
        zfar[d][1].wait_recv()
    x2[1].first()
    x2[1].second()
    x2[0].forward()
    for r in (x1, x3):
        r.rest()
        r.finish()
    integral(192, 320, 0, 384, 128)
    y1[1].forward()
    x2[1].forward()
    for r in y1:
        r.rest()
    integral(0, 512, 384, 640, 256)
    early = swapped(0, 512, 0, 640)
    x2[0].rest()
    x2[0].finish()
    y1[0].finish()
    early.wait_recv()
    amplitude(0, 512, 0, 640)
    x2[1].rest()
    x2[1].finish()
    y1[1].finish()
    integral(512, 256, 0, 512, 256)
    integral(512, 256, 512, 640, 128)
    late = [swapped(512, 256, 0, 640)]
    integral(0, ROWS, 640, ROWS, 128)
    late.append(swapped(0, ROWS, 640, ROWS))
    late[0].wait_recv()
    amplitude(512, 256, 0, 640)
    late[1].wait_recv()
    amplitude(0, ROWS, 640, ROWS)

    def store(t, h, n, cs, out, acc, hold, l, d):
        acc[t, h, :, cs] = out[0:n]
        l[t, h, :, cs] = out[3 * n:4 * n].astype(BF16)
        if h == 0:
            hold[t % 2, 0, :, cs] = out[n:2 * n]
            d[t, 1, :, cs] = out[2 * n:3 * n].astype(BF16)
        else:
            hold[t % 2, 1, :, cs] = out[2 * n:3 * n]
            d[t, 0, :, cs] = out[n:2 * n].astype(BF16)

    def product0(t, h):
        i, s = CHUNK[t // 2][h], t % 2
        lhs = amp[POS[i] * 4 * RC:(POS[i] + 1) * 4 * RC, :]

        @pl.loop(0, Q1 // 512)
        def _(n):
            o = pl.multiple_of(n * 512, 512)
            out = jnp.dot(lhs, B[:, pl.ds(o + h * Q + s * Q1, 512)], preferred_element_type=F32)
            store(t, h, RC, pl.ds(o, 512), out, acc0, hold0, l0, d0)

        if s == 1:
            rhs = ampd[pl.ds(pl.multiple_of(i % 2 * (ROWS // 2) + h * 128 + c * 128, 128), 128), :]
            out = lax.dot_general(lhs, rhs, NT, preferred_element_type=F32)
            store(t, h, RC, pl.ds(Q1, 128), out, acc0, hold0, l0, d0)

    def product1(t, h):
        b, s = 1 - t // 4, t % 4
        lhs = ampt[b * ROWS // 2:(b + 1) * ROWS // 2, :]

        @pl.loop(0, Q2 // 256)
        def _(n):
            o = pl.multiple_of(n * 256, 256)
            out = jnp.dot(lhs, A[:, pl.ds(o + s * Q1 + h * Q2, 256)], preferred_element_type=F32)
            store(t, h, 2 * RC, pl.ds(o, 256), out, acc1, hold1, l1, d1)

    class Sum:
        def __init__(self, t, width, to, product, acc, hold, l, d, rl, rd, rm):
            w = pl.ds(0, width)
            full = pl.ds(0, acc.shape[2])
            self.t, self.w, self.product = t, w, product
            self.acc, self.hold, self.l, self.rd, self.rl, self.rm = acc, hold, l, rd, rl, rm
            self.m1 = [msg(l.at[t, f, full, w], rl.at[t, f, full, w], to[f]) for f in range(2)]
            self.md = [msg(d.at[t, f, full, w], rd.at[t, f, full, w], to[f]) for f in range(2)]
            self.m2 = [msg(l.at[t, f, full, w], rm.at[t, f, full, w], to[f]) for f in range(2)]

        def lead(self):
            for f in range(2):
                self.product(self.t, f)
                go(self.m1[f], False)

        def follow(self):
            for f in (1, 0):
                go(self.md[f], False)

        def start(self):
            self.lead()
            self.follow()

        def relay(self):
            t, w = self.t, self.w
            for f in range(2):
                self.m1[f].wait_send()
                self.m1[f].wait_recv()
                self.l[t, f, :, w] = (self.hold[t % 2, f, :, w] + self.rl[t, f, :, w].astype(F32)).astype(BF16)
                go(self.m2[f])

        def total(self, h):
            t, w = self.t, self.w
            return (self.acc[t, h, :, w] + self.rm[t, h, :, w].astype(F32) + self.rd[t, 1 - h, :, w].astype(F32))

        def finish(self):
            for f in range(2):
                self.md[f].wait_send()
                self.md[f].wait_recv()
            for f in range(2):
                self.m2[f].wait_recv()

    s0 = [Sum(t, Q1 + t % 2 * 128, xs, product0, acc0, hold0, l0, d0, rl0, rd0, rm0) for t in range(8)]
    s1 = [Sum(t, Q2, ys, product1, acc1, hold1, l1, d1, rl1, rd1, rm1) for t in range(8)]

    def zmsgs(t, k, flip):
        w = (pl.ds(0, RC), s0[t].w)
        return [msg(d0.at[(t, 1 - f if flip else f) + w], rz.at[(k, t % 2, f) + w], zs[f]) for f in range(2)]

    zl = [zmsgs(t, 0, False) for t in (0, 1)]
    zm = [zmsgs(t, 1, False) for t in (2, 3)]
    zd = [zmsgs(t, 2, True) for t in (4, 5)]
    mp = [msg(d1.at[t], rp.at[t], pair) for t in range(4)]
    outs = []

    def put(src, dst):
        cp = pltpu.make_async_copy(src, dst, osem.at[len(outs)])
        cp.start()
        outs.append(cp)

    def cols(core_, o, n):
        return pl.ds(pl.multiple_of(core_ * HALF + o, 128), n)

    f0m, f1m = [], []

    def done0(t):
        s0[t].finish()
        p, s, w = t // 2, t % 2, s0[t].w
        for f in range(2):
            if p == 0:
                d0[t, f, :, w] = s0[t].total(f).astype(BF16)
                go(zl[s][f])
            elif p == 1:
                zl[s][f].wait_recv()
                d0[t, f, :, w] = (s0[t].total(f) + rz[0, s, f, :, w].astype(F32)).astype(BF16)
                go(zm[s][f])
            elif p == 2:
                d0[t, 1 - f, :, w] = s0[t].total(1 - f).astype(BF16)
                go(zd[s][f])
            else:
                zm[s][f].wait_recv()
                zd[s][f].wait_recv()
        if p == 3:
            for h in range(2):
                acc0[t, h, :, w] = (s0[t].total(h) + rz[1, s, h, :, w].astype(F32)
                                    + rz[2, s, 1 - h, :, w].astype(F32))
            f0m.append(go(msg(acc0.at[t, :, pl.ds(theirs, R), w], f0.at[s, :, :, w], core)))
            for h in range(2):
                put(acc0.at[t, h, pl.ds(mine, R), pl.ds(0, Q1)], gamma_ref.at[0, :, cols(c, h * Q + s * Q1, Q1)])
                if s == 1:
                    put(acc0.at[t, h, pl.ds(mine, R), pl.ds(Q1, 128)],
                        dens_ref.at[:, pl.ds(pl.multiple_of((c + h) * 128, 128), 128)])

    def land0(s):
        f0m[s].wait_recv()
        for h in range(2):
            put(f0.at[s, h, :, pl.ds(0, Q1)], gamma_ref.at[0, :, cols(1 - c, h * Q + s * Q1, Q1)])
        if s == 1:
            put(f0.at[s, 1 - c, :, pl.ds(Q1, 128)],
                dens_ref.at[:, pl.ds(pl.multiple_of((1 - c) * 256, 128), 128)])

    def done1(t):
        s1[t].finish()
        if t < 4:
            for h in range(2):
                d1[t, h] = s1[t].total(h).astype(BF16)
            go(mp[t])
            return
        s = t - 4
        mp[s].wait_recv()
        for h in range(2):
            acc1[t, h] = s1[t].total(h) + rp[s, h].astype(F32)
        for k in range(2):
            f1m.append(go(msg(acc1.at[t, :, pl.ds(pl.multiple_of(k * RC + theirs, 8), R)], f1.at[s, k], core)))
        for k in range(2):
            for h in range(2):
                put(acc1.at[t, h, pl.ds(pl.multiple_of(k * RC + mine, 8), R)],
                    gamma_ref.at[1 + k, :, cols(c, s * Q1 + h * Q2, Q2)])

    def land1(s):
        for k in range(2):
            f1m[s * 2 + k].wait_recv()
            for h in range(2):
                put(f1.at[s, k, h], gamma_ref.at[1 + k, :, cols(1 - c, s * Q1 + h * Q2, Q2)])

    s0[0].start()
    s1[0].start()
    s0[0].relay()
    s0[1].start()
    s1[0].relay()
    s1[1].start()
    done0(0)
    done1(0)
    for t in range(1, 8):
        if t < 7:
            s0[t + 1].lead()
            s1[t + 1].lead()
        s0[t].relay()
        s1[t].relay()
        if t < 7:
            s0[t + 1].follow()
            s1[t + 1].follow()
        if t > 1:
            done0(t - 1)
            done1(t - 1)
        if t - 2 >= 4:
            land1(t - 6)
    land0(0)
    land1(2)
    done0(7)
    done1(7)
    land0(1)
    land1(3)
    for m in sent:
        m.wait_send()
    for cp in outs:
        cp.wait()


def write(gamma_in, dens_in, gamma_ref, dens_ref, gamma_via, dens_via, sem):
    parts = [(gamma_in.at[k, pl.ds(8 * r, 8)], gamma_via.at[k, pl.ds(8 * r, 8)], gamma_ref.at[k, pl.ds(8 * r, 8)])
             for k in range(3) for r in range(3)] + [(dens_in, dens_via, dens_ref)]
    come = [pltpu.make_async_copy(p[0], p[1], sem.at[0, n]) for n, p in enumerate(parts)]
    leave = [pltpu.make_async_copy(p[1], p[2], sem.at[1, n]) for n, p in enumerate(parts)]
    for cp in come:
        cp.start()
    for cp, then in zip(come, leave):
        cp.wait()
        then.start()
    for cp in leave:
        cp.wait()


def shards(b_factors, occ_energy, vir_energy, pair_ids):
    vm = pl.BlockSpec(memory_space=pltpu.VMEM)
    V = pltpu.VMEM
    shapes = (jax.ShapeDtypeStruct((3, R, 2 * HALF), F32), jax.ShapeDtypeStruct((R, 16 * R), F32))
    anywhere = pl.BlockSpec(memory_space=pl.ANY)
    gamma, density = pl.pallas_call(
        kernel,
        out_shape=shapes,
        in_specs=[vm, vm, pl.BlockSpec(memory_space=pltpu.SMEM), anywhere],
        out_specs=(anywhere, anywhere),
        scratch_shapes=[
            V((3, R, 2 * HALF), BF16), V((ROWS, WID), BF16), V((ROWS, WID), BF16), V((3, RC, WID), F32), V((3, R, WID), F32),
            V((ROWS, ROWS), F32), V((ROWS, ROWS), F32),
            V((ROWS, ROWS), BF16), V((ROWS, ROWS), BF16), V((ROWS, ROWS), BF16),
            V((8, 2, RC, W0), F32), V((2, 2, RC, W0), F32), V((8, 2, RC, W0), BF16), V((8, 2, RC, W0), BF16),
            V((8, 2, RC, W0), BF16), V((8, 2, RC, W0), BF16), V((8, 2, RC, W0), BF16),
            V((8, 2, 2 * RC, Q2), F32), V((2, 2, 2 * RC, Q2), F32), V((8, 2, 2 * RC, Q2), BF16),
            V((8, 2, 2 * RC, Q2), BF16),
            V((8, 2, 2 * RC, Q2), BF16), V((8, 2, 2 * RC, Q2), BF16), V((8, 2, 2 * RC, Q2), BF16),
            V((3, 2, 2, RC, W0), BF16), V((4, 2, 2 * RC, Q2), BF16),
            V((2, 2, R, W0), F32), V((4, 2, 2, R, Q2), F32),
            pltpu.SemaphoreType.DMA((NMSG,)), pltpu.SemaphoreType.DMA((NMSG,)), pltpu.SemaphoreType.DMA((64,)),
        ],
        compiler_params=pltpu.CompilerParams(
            collective_id=0, has_side_effects=True, vmem_limit_bytes=61 * 2**20),
        cost_estimate=pl.CostEstimate(flops=15 * 10**9, bytes_accessed=4 * 10**6, transcendentals=0),
        name="mp2",
    )(vir_energy.reshape(1, R), occ_energy.reshape(12, 128), pair_ids, b_factors)
    return pl.pallas_call(
        write, out_shape=shapes, in_specs=[anywhere, anywhere], out_specs=(anywhere, anywhere),
        scratch_shapes=[V((3, R, 2 * HALF), F32), V((R, 16 * R), F32), pltpu.SemaphoreType.DMA((2, 10))], name="write",
    )(gamma, density)


def solution(mesh):
    in_specs = (P(None, ("row", "col"), None), P(), P(("row", "col")), P())
    out_specs = (P(None, ("row", "col"), None), P(("row", "col"), None))
    return jax.shard_map(shards, mesh=mesh, in_specs=in_specs, out_specs=out_specs, check_vma=False)
```

```python
import jax
import jax.numpy as jnp
from jax import lax
from jax.experimental import pallas as pl
from jax.experimental.pallas import tpu as pltpu
from jax.sharding import PartitionSpec as P

MESH = pl.DeviceIdType.MESH
F32, BF16 = jnp.float32, jnp.bfloat16
NT = (((1,), (1,)), ((), ()))

R = 24
RC = 2 * R
HALF = 4096
EXT = 128
WID = HALF + EXT
CUT = 2048
Q = 2048
W0 = Q // 2 + 128
ROWS = 16 * RC
NMSG = 224
Q1, Q2 = Q // 2, Q // 4
ORD = (0, 1, 3, 2)
POS = tuple(ORD.index(k) for k in range(4))
CHUNK = ((2, 2), (1, 3), (3, 1), (0, 0))


def kernel(vir_ref, occ_ref, pid_ref, b_hbm, gamma_ref, dens_ref,
           b_ref, A, B, st, snd, ip, ir, amp, ampt, ampd,
           acc0, hold0, l0, d0, rl0, rd0, rm0,
           acc1, hold1, l1, d1, rl1, rd1, rm1,
           acc2, hold2, l2, d2, rl2, rd2, rm2,
           rz, rp, f0, f1, ssem, rsem, osem):
    row, col = lax.axis_index("row"), lax.axis_index("col")
    x, y, z, c = col // 4, row % 4, (col // 2) % 2 * 4 + row // 4, col % 2

    def dev(x, y, z, c):
        return (z % 4 * 4 + y, x * 4 + z // 4 * 2 + c)

    xs = [dev((x + 1) % 4, y, z, c), dev((x + 3) % 4, y, z, c)]
    ys = [dev(x, (y + 1) % 4, z, c), dev(x, (y + 3) % 4, z, c)]
    zs = [dev(x, y, (z + 2) % 8, c), dev(x, y, (z + 6) % 8, c)]
    far = dev(x, y, (z + 4) % 8, c)
    pair = dev(x, y, z + 1 - 2 * (z % 2), c)
    core = dev(x, y, z, 1 - c)
    peers = xs + ys + zs + [far, pair, core]

    barrier = pltpu.get_barrier_semaphore()
    for p in peers:
        pl.semaphore_signal(barrier, inc=1, device_id=p, device_id_type=MESH)

    load = pltpu.make_async_copy(b_hbm, b_ref, osem.at[63])
    load.start()

    count = [0]

    def msg(src, dst, to):
        i = count[0]
        count[0] += 1
        return pltpu.make_async_remote_copy(
            src_ref=src, dst_ref=dst, send_sem=ssem.at[i], recv_sem=rsem.at[i],
            device_id=to, device_id_type=MESH)

    sent = []

    def go(m, later=True):
        m.start()
        if later:
            sent.append(m)
        return m

    lane = lax.broadcasted_iota(jnp.int32, (R, EXT), 1)
    e = vir_ref[...]
    diag = lax.broadcasted_iota(jnp.int32, (R, R), 0) == lax.broadcasted_iota(jnp.int32, (R, R), 1)
    e_hi = jnp.sum(jnp.where(diag, (e >> 6).astype(F32), 0.0), axis=1, keepdims=True) * (64.0 / 1024.0)
    e_lo = jnp.sum(jnp.where(diag, (e & 63).astype(F32), 0.0), axis=1, keepdims=True) * (1.0 / 1024.0)
    occ = occ_ref[...]
    place = lax.broadcasted_iota(jnp.int32, occ.shape, 0) * occ.shape[1] + lax.broadcasted_iota(
        jnp.int32, occ.shape, 1)

    def level(k):
        picked = jnp.where(place == pid_ref[k], occ.astype(F32), 0.0)
        return jnp.sum(jnp.sum(picked, axis=1, keepdims=True), axis=0, keepdims=True)

    zero = jnp.zeros((R, EXT), F32)
    exts = [jnp.where(lane == 0, e_hi, jnp.where(lane == 1, e_lo, jnp.where(
        lane < 4, 1.0, jnp.where(lane < 6, -1.0, zero))))]
    for k in range(2):
        s = level(0) + level(1 + k)
        s_hi = jnp.floor(s * (1.0 / 64.0))
        s_lo = s - s_hi * 64.0
        exts.append(jnp.where(lane < 2, 1.0, jnp.where(lane == 2, e_hi, jnp.where(lane == 3, e_lo, jnp.where(
            lane == 4, s_hi * (64.0 / 1024.0), jnp.where(lane == 5, s_lo * (1.0 / 1024.0), zero))))))

    mine = pl.multiple_of(c * R, 8)
    theirs = pl.multiple_of((1 - c) * R, 8)

    load.wait()

    @pl.loop(0, 3)
    def _(m):
        @pl.loop(0, HALF // 512)
        def _(n):
            o = pl.multiple_of(n * 512, 128)
            st[m, pl.ds(mine, R), pl.ds(o, 512)] = b_ref[m, :, pl.ds(pl.multiple_of(c * HALF + o, 128), 512)].astype(F32)
            snd[m, :, pl.ds(o, 512)] = b_ref[m, :, pl.ds(pl.multiple_of((1 - c) * HALF + o, 128), 512)].astype(F32)

    for m in range(3):
        st[m, pl.ds(mine, R), HALF:] = exts[m]
        snd[m, :, HALF:] = exts[m]

    pl.semaphore_wait(barrier, len(peers))
    swap = [go(msg(snd.at[m], st.at[m, pl.ds(mine, R)], core)) for m in range(3)]

    def arow(i, j):
        return (POS[i] * 4 + POS[j]) * RC

    def brow(b, j):
        return (b * 4 + POS[j]) * 2 * RC

    H = [pl.ds(0, CUT), pl.ds(CUT, WID - CUT)]
    H4 = [pl.ds(0, 1024), pl.ds(1024, 1024), pl.ds(2048, 1024), pl.ds(3072, WID - 3072)]

    class Ring:
        def __init__(self, buf, at, n, to, cut):
            rows = lambda s: pl.ds(at[s], n)
            self.own = [[msg(buf.at[rows(0), cut[h]], buf.at[rows((3, 1)[d]), cut[h]], to[d]) for h in range(2)]
                        for d in range(2)]
            self.fwd = [msg(buf.at[rows((3, 1)[d]), cut[d]], buf.at[rows(2), cut[d]], to[d]) for d in range(2)]

        def first(self):
            for d in range(2):
                go(self.own[d][d])

        def second(self):
            for d in range(2):
                go(self.own[d][1 - d])

        def forward(self, ds=(0, 1)):
            for d in ds:
                self.own[d][d].wait_recv()
                go(self.fwd[d])

        def rest(self):
            for d in range(2):
                self.own[d][1 - d].wait_recv()

        def finish(self):
            for d in range(2):
                self.fwd[d].wait_recv()

    zown = [[msg(A.at[pl.ds(0, RC), H[h]], A.at[pl.ds(arow((3, 1)[d], 0), RC), H[h]], zs[d]) for h in range(2)]
            for d in range(2)]
    zfar = [[msg(A.at[pl.ds(arow((3, 1)[d], 0), RC), H4[2 * d + p]], A.at[pl.ds(arow(2, 0), RC), H4[2 * d + p]], zs[d])
             for p in range(2)] for d in range(2)]
    xr = [Ring(A, [arow(i, j) for j in range(4)], RC, xs, H) for i in (0, 1, 3)]
    x0, x1, x3 = xr
    x2 = [Ring(A, [arow(2, j) for j in range(4)], RC, xs, [H4[p], H4[2 + p]]) for p in range(2)]
    y0 = Ring(B, [brow(0, j) for j in range(4)], 2 * RC, ys, H)
    y1 = [Ring(B, [brow(1, j) for j in range(4)], 2 * RC, ys, [H4[p], H4[2 + p]]) for p in range(2)]
    pr = [[msg(B.at[pl.ds(0, 2 * RC), H4[p + q]], B.at[pl.ds(brow(1, 0), 2 * RC), H4[p + q]], pair) for q in (0, 2)]
          for p in range(2)]

    def integral(r, n, o0, o1, w):
        @pl.loop(0, (o1 - o0) // w)
        def _(k):
            o = pl.ds(pl.multiple_of(o0 + k * w, 128), w)
            ip[r:r + n, o] = lax.dot_general(A[r:r + n, 0:HALF], B[o, 0:HALF], NT, preferred_element_type=F32)

    def swapped(r, n, o0, o1):
        part = (pl.ds(r, n), pl.ds(o0, o1 - o0))
        return go(msg(ip.at[part], ir.at[part], core))

    def slot(s):
        i, j = ORD[s // 4], ORD[s % 4]
        return i % 2 * (ROWS // 2) + ((x + j) % 4 * 2 + (z + 2 * i) % 8 // 4) * RC

    def amplitude(r, n, o0, o1):
        @pl.loop(0, (o1 - o0) // 128)
        def _(k):
            o = pl.ds(pl.multiple_of(o0 + k * 128, 128), 128)
            rows = pl.ds(r, n)
            den = lax.dot_general(A[rows, HALF:], B[o, HALF:], NT, preferred_element_type=F32)
            t = ((ip[rows, o] + ir[rows, o]) / (0.0 - den)).astype(BF16)
            amp[rows, o] = t
            ampt[o, rows] = t.astype(F32).T.astype(BF16)
            for s in range(16):
                lo, hi = max(r, s * RC), min(r + n, s * RC + RC)
                if lo < hi:
                    ampd[pl.ds(pl.multiple_of(slot(s) + lo - s * RC, 16), hi - lo), o] = t[lo - r:hi - r]

    def settle(buf, to, m):
        swap[m].wait_recv()

        @pl.loop(0, 3)
        def _(n):
            o = pl.ds(pl.multiple_of(n * 1408, 128), 1408)
            buf[to:to + RC, o] = st[m, :, o].astype(BF16)

    settle(A, 0, 0)
    for d in range(2):
        go(zown[d][d])
    x0.first()
    for d in range(2):
        go(zown[d][1 - d])
    x0.second()
    for k in range(2):
        settle(B, k * RC, 1 + k)
    y0.first()
    y0.second()
    x0.forward()
    for d in range(2):
        zown[d][d].wait_recv()
    for q in range(2):
        go(pr[0][q])
    go(x3.own[0][0])
    go(x1.own[1][1])
    go(x3.own[1][0])
    go(x1.own[0][1])
    y0.forward()
    for d in range(2):
        zown[d][1 - d].wait_recv()
    for q in range(2):
        go(pr[1][q])
    go(x3.own[0][1])
    go(x1.own[1][0])
    go(x3.own[1][1])
    go(x1.own[0][0])
    x3.forward((0,))
    x1.forward((1,))
    for q in range(2):
        pr[0][q].wait_recv()
    y1[0].first()
    y1[0].second()
    for d in range(2):
        go(zfar[d][0])
    for r in (x0, y0):
        r.rest()
        r.finish()
    integral(0, 192, 0, 384, 128)
    x3.forward((1,))
    x1.forward((0,))
    for q in range(2):
        pr[1][q].wait_recv()
    y1[1].first()
    y1[1].second()
    for d in range(2):
        go(zfar[d][1])
    for d in range(2):
        zfar[d][0].wait_recv()
    x2[0].first()
    x2[0].second()
    y1[0].forward()
    for d in range(2):
        zfar[d][1].wait_recv()
    x2[1].first()
    x2[1].second()
    x2[0].forward()
    for r in (x1, x3):
        r.rest()
        r.finish()
    integral(192, 320, 0, 384, 128)
    y1[1].forward()
    x2[1].forward()
    for r in y1:
        r.rest()
    integral(0, 512, 384, 640, 256)
    early = swapped(0, 512, 0, 640)
    x2[0].rest()
    x2[0].finish()
    y1[0].finish()
    early.wait_recv()
    amplitude(0, 512, 0, 640)
    x2[1].rest()
    x2[1].finish()
    y1[1].finish()
    integral(512, 256, 0, 512, 256)
    integral(512, 256, 512, 640, 128)
    late = [swapped(512, 256, 0, 640)]
    integral(0, ROWS, 640, ROWS, 128)
    late.append(swapped(0, ROWS, 640, ROWS))
    late[0].wait_recv()
    amplitude(512, 256, 0, 640)
    late[1].wait_recv()
    amplitude(0, ROWS, 640, ROWS)

    def store(t, h, n, cs, out, acc, hold, l, d):
        acc[t, h, :, cs] = out[0:n]
        l[t, h, :, cs] = out[3 * n:4 * n].astype(BF16)
        if h == 0:
            hold[t % 2, 0, :, cs] = out[n:2 * n]
            d[t, 1, :, cs] = out[2 * n:3 * n].astype(BF16)
        else:
            hold[t % 2, 1, :, cs] = out[2 * n:3 * n]
            d[t, 0, :, cs] = out[n:2 * n].astype(BF16)

    def product0(t, h):
        i, s = CHUNK[t // 2][h], t % 2
        lhs = amp[POS[i] * 4 * RC:(POS[i] + 1) * 4 * RC, :]

        @pl.loop(0, Q1 // 512)
        def _(n):
            o = pl.multiple_of(n * 512, 512)
            out = jnp.dot(lhs, B[:, pl.ds(o + h * Q + s * Q1, 512)], preferred_element_type=F32)
            store(t, h, RC, pl.ds(o, 512), out, acc0, hold0, l0, d0)

        if t == 7:
            store(t, h, RC, pl.ds(Q1, 128), s2.total(h), acc0, hold0, l0, d0)

    def product1(t, h):
        b, s = 1 - t // 4, t % 4
        lhs = ampt[b * ROWS // 2:(b + 1) * ROWS // 2, :]

        @pl.loop(0, Q2 // 256)
        def _(n):
            o = pl.multiple_of(n * 256, 256)
            out = jnp.dot(lhs, A[:, pl.ds(o + s * Q1 + h * Q2, 256)], preferred_element_type=F32)
            store(t, h, 2 * RC, pl.ds(o, 256), out, acc1, hold1, l1, d1)

    def product2(t, h):
        n = 4 * RC
        for i in range(4):
            rhs = ampd[pl.ds(pl.multiple_of(i % 2 * (ROWS // 2) + h * 128 + c * 128, 128), 128), :]
            out = lax.dot_general(amp[POS[i] * n:(POS[i] + 1) * n, :], rhs, NT, preferred_element_type=F32)
            if i == 0:
                acc2[t, h] = out
            elif i == 2:
                l2[t, h] = out.astype(BF16)
            elif i == 1 + 2 * h:
                hold2[t, h] = out
            else:
                d2[t, 1 - h] = out.astype(BF16)

    class Sum:
        def __init__(self, t, width, to, product, acc, hold, l, d, rl, rd, rm):
            w = pl.ds(0, width)
            full = pl.ds(0, acc.shape[2])
            self.t, self.w, self.product = t, w, product
            self.acc, self.hold, self.l, self.rd, self.rl, self.rm = acc, hold, l, rd, rl, rm
            self.m1 = [msg(l.at[t, f, full, w], rl.at[t, f, full, w], to[f]) for f in range(2)]
            self.md = [msg(d.at[t, f, full, w], rd.at[t, f, full, w], to[f]) for f in range(2)]
            self.m2 = [msg(l.at[t, f, full, w], rm.at[t, f, full, w], to[f]) for f in range(2)]

        def lead(self):
            for f in range(2):
                self.product(self.t, f)
                go(self.m1[f], False)

        def follow(self):
            for f in (1, 0):
                go(self.md[f], False)

        def start(self):
            self.lead()
            self.follow()

        def relay(self):
            t, w = self.t, self.w
            for f in range(2):
                self.m1[f].wait_send()
                self.m1[f].wait_recv()
                self.l[t, f, :, w] = (self.hold[t % 2, f, :, w] + self.rl[t, f, :, w].astype(F32)).astype(BF16)
                go(self.m2[f])

        def total(self, h):
            t, w = self.t, self.w
            return (self.acc[t, h, :, w] + self.rm[t, h, :, w].astype(F32) + self.rd[t, 1 - h, :, w].astype(F32))

        def finish(self):
            for f in range(2):
                self.md[f].wait_send()
                self.md[f].wait_recv()
            for f in range(2):
                self.m2[f].wait_recv()

    s2 = Sum(0, 128, zs, product2, acc2, hold2, l2, d2, rl2, rd2, rm2)
    s0 = [Sum(t, Q1 + t // 7 * 128, xs, product0, acc0, hold0, l0, d0, rl0, rd0, rm0) for t in range(8)]
    s1 = [Sum(t, Q2, ys, product1, acc1, hold1, l1, d1, rl1, rd1, rm1) for t in range(8)]

    def zmsgs(t, k, flip):
        w = (pl.ds(0, RC), s0[t].w)
        return [msg(d0.at[(t, 1 - f if flip else f) + w], rz.at[(k, t % 2, f) + w], zs[f]) for f in range(2)]

    zl = [zmsgs(t, 0, False) for t in (0, 1)]
    zm = [zmsgs(t, 1, False) for t in (2, 3)]
    zd = [zmsgs(t, 2, True) for t in (4, 5)]
    mp = [msg(d1.at[t], rp.at[t], pair) for t in range(4)]
    outs = []

    def put(src, dst):
        cp = pltpu.make_async_copy(src, dst, osem.at[len(outs)])
        cp.start()
        outs.append(cp)

    def cols(core_, o, n):
        return pl.ds(pl.multiple_of(core_ * HALF + o, 128), n)

    f0m, f1m = [], []

    def done0(t):
        s0[t].finish()
        p, s, w = t // 2, t % 2, s0[t].w
        for f in range(2):
            if p == 0:
                d0[t, f, :, w] = s0[t].total(f).astype(BF16)
                go(zl[s][f])
            elif p == 1:
                zl[s][f].wait_recv()
                d0[t, f, :, w] = (s0[t].total(f) + rz[0, s, f, :, w].astype(F32)).astype(BF16)
                go(zm[s][f])
            elif p == 2:
                d0[t, 1 - f, :, w] = s0[t].total(1 - f).astype(BF16)
                go(zd[s][f])
            else:
                zm[s][f].wait_recv()
                zd[s][f].wait_recv()
        if p == 3:
            for h in range(2):
                acc0[t, h, :, w] = s0[t].total(h)
                acc0[t, h, :, 0:Q1] += rz[1, s, h].astype(F32) + rz[2, s, 1 - h].astype(F32)
            f0m.append(go(msg(acc0.at[t, :, pl.ds(theirs, R), w], f0.at[s, :, :, w], core)))
            for h in range(2):
                put(acc0.at[t, h, pl.ds(mine, R), pl.ds(0, Q1)], gamma_ref.at[0, :, cols(c, h * Q + s * Q1, Q1)])
                if s == 1:
                    put(acc0.at[t, h, pl.ds(mine, R), pl.ds(Q1, 128)],
                        dens_ref.at[:, pl.ds(pl.multiple_of((c + h) * 128, 128), 128)])

    def land0(s):
        f0m[s].wait_recv()
        for h in range(2):
            put(f0.at[s, h, :, pl.ds(0, Q1)], gamma_ref.at[0, :, cols(1 - c, h * Q + s * Q1, Q1)])
        if s == 1:
            put(f0.at[s, 1 - c, :, pl.ds(Q1, 128)],
                dens_ref.at[:, pl.ds(pl.multiple_of((1 - c) * 256, 128), 128)])

    def done1(t):
        s1[t].finish()
        if t < 4:
            for h in range(2):
                d1[t, h] = s1[t].total(h).astype(BF16)
            go(mp[t])
            return
        s = t - 4
        mp[s].wait_recv()
        for h in range(2):
            acc1[t, h] = s1[t].total(h) + rp[s, h].astype(F32)
        for k in range(2):
            f1m.append(go(msg(acc1.at[t, :, pl.ds(pl.multiple_of(k * RC + theirs, 8), R)], f1.at[s, k], core)))
        for k in range(2):
            for h in range(2):
                put(acc1.at[t, h, pl.ds(pl.multiple_of(k * RC + mine, 8), R)],
                    gamma_ref.at[1 + k, :, cols(c, s * Q1 + h * Q2, Q2)])

    def land1(s):
        for k in range(2):
            f1m[s * 2 + k].wait_recv()
            for h in range(2):
                put(f1.at[s, k, h], gamma_ref.at[1 + k, :, cols(1 - c, s * Q1 + h * Q2, Q2)])

    s0[0].start()
    s1[0].start()
    s2.start()
    s0[0].relay()
    s0[1].start()
    s1[0].relay()
    s2.relay()
    s1[1].start()
    done0(0)
    done1(0)
    for t in range(1, 8):
        if t < 7:
            s0[t + 1].lead()
            s1[t + 1].lead()
        s0[t].relay()
        s1[t].relay()
        if t < 7:
            s0[t + 1].follow()
            s1[t + 1].follow()
        if t > 1:
            done0(t - 1)
            done1(t - 1)
        if t - 2 >= 4:
            land1(t - 6)
        if t == 3:
            s2.finish()
    land0(0)
    land1(2)
    done0(7)
    done1(7)
    land0(1)
    land1(3)
    for m in sent:
        m.wait_send()
    for cp in outs:
        cp.wait()


def write(gamma_in, dens_in, gamma_ref, dens_ref, gamma_via, dens_via, sem):
    parts = [(gamma_in.at[k, pl.ds(8 * r, 8)], gamma_via.at[k, pl.ds(8 * r, 8)], gamma_ref.at[k, pl.ds(8 * r, 8)])
             for k in range(3) for r in range(3)] + [(dens_in, dens_via, dens_ref)]
    come = [pltpu.make_async_copy(p[0], p[1], sem.at[0, n]) for n, p in enumerate(parts)]
    leave = [pltpu.make_async_copy(p[1], p[2], sem.at[1, n]) for n, p in enumerate(parts)]
    for cp in come:
        cp.start()
    for cp, then in zip(come, leave):
        cp.wait()
        then.start()
    for cp in leave:
        cp.wait()


def shards(b_factors, occ_energy, vir_energy, pair_ids):
    vm = pl.BlockSpec(memory_space=pltpu.VMEM)
    V = pltpu.VMEM
    shapes = (jax.ShapeDtypeStruct((3, R, 2 * HALF), F32), jax.ShapeDtypeStruct((R, 16 * R), F32))
    anywhere = pl.BlockSpec(memory_space=pl.ANY)
    gamma, density = pl.pallas_call(
        kernel,
        out_shape=shapes,
        in_specs=[vm, vm, pl.BlockSpec(memory_space=pltpu.SMEM), anywhere],
        out_specs=(anywhere, anywhere),
        scratch_shapes=[
            V((3, R, 2 * HALF), BF16), V((ROWS, WID), BF16), V((ROWS, WID), BF16), V((3, RC, WID), F32), V((3, R, WID), F32),
            V((ROWS, ROWS), F32), V((ROWS, ROWS), F32),
            V((ROWS, ROWS), BF16), V((ROWS, ROWS), BF16), V((ROWS, ROWS), BF16),
            V((8, 2, RC, W0), F32), V((2, 2, RC, W0), F32), V((8, 2, RC, W0), BF16), V((8, 2, RC, W0), BF16),
            V((8, 2, RC, W0), BF16), V((8, 2, RC, W0), BF16), V((8, 2, RC, W0), BF16),
            V((8, 2, 2 * RC, Q2), F32), V((2, 2, 2 * RC, Q2), F32), V((8, 2, 2 * RC, Q2), BF16),
            V((8, 2, 2 * RC, Q2), BF16),
            V((8, 2, 2 * RC, Q2), BF16), V((8, 2, 2 * RC, Q2), BF16), V((8, 2, 2 * RC, Q2), BF16),
            V((1, 2, 4 * RC, 128), F32), V((1, 2, 4 * RC, 128), F32), V((1, 2, 4 * RC, 128), BF16),
            V((1, 2, 4 * RC, 128), BF16),
            V((1, 2, 4 * RC, 128), BF16), V((1, 2, 4 * RC, 128), BF16), V((1, 2, 4 * RC, 128), BF16),
            V((3, 2, 2, RC, Q1), BF16), V((4, 2, 2 * RC, Q2), BF16),
            V((2, 2, R, W0), F32), V((4, 2, 2, R, Q2), F32),
            pltpu.SemaphoreType.DMA((NMSG,)), pltpu.SemaphoreType.DMA((NMSG,)), pltpu.SemaphoreType.DMA((64,)),
        ],
        compiler_params=pltpu.CompilerParams(
            collective_id=0, has_side_effects=True, vmem_limit_bytes=61 * 2**20),
        cost_estimate=pl.CostEstimate(flops=15 * 10**9, bytes_accessed=4 * 10**6, transcendentals=0),
        name="mp2",
    )(vir_energy.reshape(1, R), occ_energy.reshape(12, 128), pair_ids, b_factors)
    return pl.pallas_call(
        write, out_shape=shapes, in_specs=[anywhere, anywhere], out_specs=(anywhere, anywhere),
        scratch_shapes=[V((3, R, 2 * HALF), F32), V((R, 16 * R), F32), pltpu.SemaphoreType.DMA((2, 10))], name="write",
    )(gamma, density)


def solution(mesh):
    in_specs = (P(None, ("row", "col"), None), P(), P(("row", "col")), P())
    out_specs = (P(None, ("row", "col"), None), P(("row", "col"), None))
    return jax.shard_map(shards, mesh=mesh, in_specs=in_specs, out_specs=out_specs, check_vma=False)
```

```python
import jax
import jax.numpy as jnp
from jax import lax
from jax.experimental import pallas as pl
from jax.experimental.pallas import tpu as pltpu
from jax.sharding import PartitionSpec as P

MESH = pl.DeviceIdType.MESH
F32, BF16 = jnp.float32, jnp.bfloat16
NT = (((1,), (1,)), ((), ()))

R = 24
RC = 2 * R
HALF = 4096
EXT = 128
WID = HALF + EXT
CUT = 2048
Q = 2048
W0 = Q // 2 + 128
ROWS = 16 * RC
NMSG = 224
Q1, Q2 = Q // 2, Q // 4
ORD = (0, 1, 3, 2)
POS = tuple(ORD.index(k) for k in range(4))
CHUNK = ((2, 2), (1, 3), (3, 1), (0, 0))


def kernel(vir_ref, occ_ref, pid_ref, b_hbm, gamma_ref, dens_ref,
           b_ref, A, B, st, snd, ip, ir, amp, ampt, ampd,
           acc0, hold0, l0, d0, rl0, rd0, rm0,
           acc1, hold1, l1, d1, rl1, rd1, rm1,
           acc2, hold2, l2, d2, rl2, rd2, rm2,
           rz, rp, f0, f1, ssem, rsem, osem):
    row, col = lax.axis_index("row"), lax.axis_index("col")
    x, y, z, c = col // 4, row % 4, (col // 2) % 2 * 4 + row // 4, col % 2

    def dev(x, y, z, c):
        return (z % 4 * 4 + y, x * 4 + z // 4 * 2 + c)

    xs = [dev((x + 1) % 4, y, z, c), dev((x + 3) % 4, y, z, c)]
    ys = [dev(x, (y + 1) % 4, z, c), dev(x, (y + 3) % 4, z, c)]
    zs = [dev(x, y, (z + 2) % 8, c), dev(x, y, (z + 6) % 8, c)]
    far = dev(x, y, (z + 4) % 8, c)
    pair = dev(x, y, z + 1 - 2 * (z % 2), c)
    core = dev(x, y, z, 1 - c)
    peers = xs + ys + zs + [far, pair, core]

    barrier = pltpu.get_barrier_semaphore()
    for p in peers:
        pl.semaphore_signal(barrier, inc=1, device_id=p, device_id_type=MESH)

    load = pltpu.make_async_copy(b_hbm, b_ref, osem.at[63])
    load.start()

    count = [0]

    def msg(src, dst, to):
        i = count[0]
        count[0] += 1
        return pltpu.make_async_remote_copy(
            src_ref=src, dst_ref=dst, send_sem=ssem.at[i], recv_sem=rsem.at[i],
            device_id=to, device_id_type=MESH)

    sent = []

    def go(m, later=True):
        m.start()
        if later:
            sent.append(m)
        return m

    lane = lax.broadcasted_iota(jnp.int32, (R, EXT), 1)
    e = vir_ref[...]
    diag = lax.broadcasted_iota(jnp.int32, (R, R), 0) == lax.broadcasted_iota(jnp.int32, (R, R), 1)
    e_hi = jnp.sum(jnp.where(diag, (e >> 6).astype(F32), 0.0), axis=1, keepdims=True) * (64.0 / 1024.0)
    e_lo = jnp.sum(jnp.where(diag, (e & 63).astype(F32), 0.0), axis=1, keepdims=True) * (1.0 / 1024.0)
    occ = occ_ref[...]
    place = lax.broadcasted_iota(jnp.int32, occ.shape, 0) * occ.shape[1] + lax.broadcasted_iota(
        jnp.int32, occ.shape, 1)

    def level(k):
        picked = jnp.where(place == pid_ref[k], occ.astype(F32), 0.0)
        return jnp.sum(jnp.sum(picked, axis=1, keepdims=True), axis=0, keepdims=True)

    zero = jnp.zeros((R, EXT), F32)
    exts = [jnp.where(lane == 0, e_hi, jnp.where(lane == 1, e_lo, jnp.where(
        lane < 4, 1.0, jnp.where(lane < 6, -1.0, zero))))]
    for k in range(2):
        s = level(0) + level(1 + k)
        s_hi = jnp.floor(s * (1.0 / 64.0))
        s_lo = s - s_hi * 64.0
        exts.append(jnp.where(lane < 2, 1.0, jnp.where(lane == 2, e_hi, jnp.where(lane == 3, e_lo, jnp.where(
            lane == 4, s_hi * (64.0 / 1024.0), jnp.where(lane == 5, s_lo * (1.0 / 1024.0), zero))))))

    mine = pl.multiple_of(c * R, 8)
    theirs = pl.multiple_of((1 - c) * R, 8)

    load.wait()

    @pl.loop(0, 3)
    def _(m):
        @pl.loop(0, HALF // 512)
        def _(n):
            o = pl.multiple_of(n * 512, 128)
            st[m, pl.ds(mine, R), pl.ds(o, 512)] = b_ref[m, :, pl.ds(pl.multiple_of(c * HALF + o, 128), 512)].astype(F32)
            snd[m, :, pl.ds(o, 512)] = b_ref[m, :, pl.ds(pl.multiple_of((1 - c) * HALF + o, 128), 512)].astype(F32)

    for m in range(3):
        st[m, pl.ds(mine, R), HALF:] = exts[m]
        snd[m, :, HALF:] = exts[m]

    pl.semaphore_wait(barrier, len(peers))
    swap = [go(msg(snd.at[m], st.at[m, pl.ds(mine, R)], core)) for m in range(3)]

    def arow(i, j):
        return (POS[i] * 4 + POS[j]) * RC

    def brow(b, j):
        return (b * 4 + POS[j]) * 2 * RC

    H = [pl.ds(0, CUT), pl.ds(CUT, WID - CUT)]
    H4 = [pl.ds(0, 1024), pl.ds(1024, 1024), pl.ds(2048, 1024), pl.ds(3072, WID - 3072)]

    class Ring:
        def __init__(self, buf, at, n, to, cut):
            rows = lambda s: pl.ds(at[s], n)
            self.own = [[msg(buf.at[rows(0), cut[h]], buf.at[rows((3, 1)[d]), cut[h]], to[d]) for h in range(2)]
                        for d in range(2)]
            self.fwd = [msg(buf.at[rows((3, 1)[d]), cut[d]], buf.at[rows(2), cut[d]], to[d]) for d in range(2)]

        def first(self):
            for d in range(2):
                go(self.own[d][d])

        def second(self):
            for d in range(2):
                go(self.own[d][1 - d])

        def forward(self, ds=(0, 1)):
            for d in ds:
                self.own[d][d].wait_recv()
                go(self.fwd[d])

        def rest(self):
            for d in range(2):
                self.own[d][1 - d].wait_recv()

        def finish(self):
            for d in range(2):
                self.fwd[d].wait_recv()

    zown = [[msg(A.at[pl.ds(0, RC), H[h]], A.at[pl.ds(arow((3, 1)[d], 0), RC), H[h]], zs[d]) for h in range(2)]
            for d in range(2)]
    zfar = [[msg(A.at[pl.ds(arow((3, 1)[d], 0), RC), H4[2 * d + p]], A.at[pl.ds(arow(2, 0), RC), H4[2 * d + p]], zs[d])
             for p in range(2)] for d in range(2)]
    xr = [Ring(A, [arow(i, j) for j in range(4)], RC, xs, H) for i in (0, 1, 3)]
    x0, x1, x3 = xr
    x2 = [Ring(A, [arow(2, j) for j in range(4)], RC, xs, [H4[p], H4[2 + p]]) for p in range(2)]
    y0 = Ring(B, [brow(0, j) for j in range(4)], 2 * RC, ys, H)
    y1 = [Ring(B, [brow(1, j) for j in range(4)], 2 * RC, ys, [H4[p], H4[2 + p]]) for p in range(2)]
    pr = [[msg(B.at[pl.ds(0, 2 * RC), H4[p + q]], B.at[pl.ds(brow(1, 0), 2 * RC), H4[p + q]], pair) for q in (0, 2)]
          for p in range(2)]

    def integral(r, n, o0, o1, w):
        @pl.loop(0, (o1 - o0) // w)
        def _(k):
            o = pl.ds(pl.multiple_of(o0 + k * w, 128), w)
            ip[r:r + n, o] = lax.dot_general(A[r:r + n, 0:HALF], B[o, 0:HALF], NT, preferred_element_type=F32)

    def swapped(r, n, o0, o1):
        part = (pl.ds(r, n), pl.ds(o0, o1 - o0))
        return go(msg(ip.at[part], ir.at[part], core))

    def slot(s):
        i, j = ORD[s // 4], ORD[s % 4]
        return i % 2 * (ROWS // 2) + ((x + j) % 4 * 2 + (z + 2 * i) % 8 // 4) * RC

    def amplitude(r, n, o0, o1):
        @pl.loop(0, (o1 - o0) // 128)
        def _(k):
            o = pl.ds(pl.multiple_of(o0 + k * 128, 128), 128)
            rows = pl.ds(r, n)
            den = lax.dot_general(A[rows, HALF:], B[o, HALF:], NT, preferred_element_type=F32)
            t = ((ip[rows, o] + ir[rows, o]) / (0.0 - den)).astype(BF16)
            amp[rows, o] = t
            ampt[o, rows] = t.astype(F32).T.astype(BF16)
            for s in range(16):
                lo, hi = max(r, s * RC), min(r + n, s * RC + RC)
                if lo < hi:
                    ampd[pl.ds(pl.multiple_of(slot(s) + lo - s * RC, 16), hi - lo), o] = t[lo - r:hi - r]

    def settle(buf, to, m):
        swap[m].wait_recv()

        @pl.loop(0, 3)
        def _(n):
            o = pl.ds(pl.multiple_of(n * 1408, 128), 1408)
            buf[to:to + RC, o] = st[m, :, o].astype(BF16)

    settle(A, 0, 0)
    for d in range(2):
        go(zown[d][d])
    x0.first()
    for d in range(2):
        go(zown[d][1 - d])
    x0.second()
    for k in range(2):
        settle(B, k * RC, 1 + k)
    for q in range(2):
        go(pr[0][q])
    y0.first()
    y0.second()
    x0.forward()
    for d in range(2):
        zown[d][d].wait_recv()
    for q in range(2):
        go(pr[1][q])
    go(x3.own[0][0])
    go(x1.own[1][1])
    go(x3.own[1][0])
    go(x1.own[0][1])
    y0.forward()
    for d in range(2):
        zown[d][1 - d].wait_recv()
    go(x3.own[0][1])
    go(x1.own[1][0])
    go(x3.own[1][1])
    go(x1.own[0][0])
    x3.forward((0,))
    x1.forward((1,))
    for q in range(2):
        pr[0][q].wait_recv()
    y1[0].first()
    y1[0].second()
    for d in range(2):
        go(zfar[d][0])
    for r in (x0, y0):
        r.rest()
        r.finish()
    integral(0, 192, 0, 256, 256)
    integral(0, 192, 256, 384, 128)
    x3.forward((1,))
    x1.forward((0,))
    for q in range(2):
        pr[1][q].wait_recv()
    y1[1].first()
    y1[1].second()
    for d in range(2):
        go(zfar[d][1])
    for d in range(2):
        zfar[d][0].wait_recv()
    x2[0].first()
    x2[0].second()
    y1[0].forward()
    for d in range(2):
        zfar[d][1].wait_recv()
    x2[1].first()
    x2[1].second()
    x2[0].forward()
    for r in (x1, x3):
        r.rest()
        r.finish()
    integral(192, 320, 0, 256, 256)
    integral(192, 320, 256, 384, 128)
    y1[1].forward()
    x2[1].forward()
    for r in y1:
        r.rest()
    integral(0, 512, 384, 640, 256)
    early = swapped(0, 512, 0, 640)
    x2[0].rest()
    x2[0].finish()
    y1[0].finish()
    early.wait_recv()
    amplitude(0, 512, 0, 640)
    x2[1].rest()
    x2[1].finish()
    y1[1].finish()
    integral(512, 256, 0, 512, 256)
    integral(512, 256, 512, 640, 128)
    late = [swapped(512, 256, 0, 640)]
    integral(0, ROWS, 640, ROWS, 128)
    late.append(swapped(0, ROWS, 640, ROWS))
    late[0].wait_recv()
    amplitude(512, 256, 0, 640)
    late[1].wait_recv()
    amplitude(0, ROWS, 640, ROWS)

    def store(t, h, n, cs, out, acc, hold, l, d):
        acc[t, h, :, cs] = out[0:n]
        l[t, h, :, cs] = out[3 * n:4 * n].astype(BF16)
        if h == 0:
            hold[t % 2, 0, :, cs] = out[n:2 * n]
            d[t, 1, :, cs] = out[2 * n:3 * n].astype(BF16)
        else:
            hold[t % 2, 1, :, cs] = out[2 * n:3 * n]
            d[t, 0, :, cs] = out[n:2 * n].astype(BF16)

    def product0(t, h):
        i, s = CHUNK[t // 2][h], t % 2
        lhs = amp[POS[i] * 4 * RC:(POS[i] + 1) * 4 * RC, :]

        @pl.loop(0, Q1 // 512)
        def _(n):
            o = pl.multiple_of(n * 512, 512)
            out = jnp.dot(lhs, B[:, pl.ds(o + h * Q + s * Q1, 512)], preferred_element_type=F32)
            store(t, h, RC, pl.ds(o, 512), out, acc0, hold0, l0, d0)

        if t == 7:
            store(t, h, RC, pl.ds(Q1, 128), s2.total(h), acc0, hold0, l0, d0)

    def product1(t, h):
        b, s = 1 - t // 4, t % 4
        lhs = ampt[b * ROWS // 2:(b + 1) * ROWS // 2, :]

        @pl.loop(0, Q2 // 256)
        def _(n):
            o = pl.multiple_of(n * 256, 256)
            out = jnp.dot(lhs, A[:, pl.ds(o + s * Q1 + h * Q2, 256)], preferred_element_type=F32)
            store(t, h, 2 * RC, pl.ds(o, 256), out, acc1, hold1, l1, d1)

    def product2(t, h):
        n = 4 * RC
        for i in range(4):
            rhs = ampd[pl.ds(pl.multiple_of(i % 2 * (ROWS // 2) + h * 128 + c * 128, 128), 128), :]
            out = lax.dot_general(amp[POS[i] * n:(POS[i] + 1) * n, :], rhs, NT, preferred_element_type=F32)
            if i == 0:
                acc2[t, h] = out
            elif i == 2:
                l2[t, h] = out.astype(BF16)
            elif i == 1 + 2 * h:
                hold2[t, h] = out
            else:
                d2[t, 1 - h] = out.astype(BF16)

    class Sum:
        def __init__(self, t, width, to, product, acc, hold, l, d, rl, rd, rm):
            w = pl.ds(0, width)
            full = pl.ds(0, acc.shape[2])
            self.t, self.w, self.product = t, w, product
            self.acc, self.hold, self.l, self.rd, self.rl, self.rm = acc, hold, l, rd, rl, rm
            self.m1 = [msg(l.at[t, f, full, w], rl.at[t, f, full, w], to[f]) for f in range(2)]
            self.md = [msg(d.at[t, f, full, w], rd.at[t, f, full, w], to[f]) for f in range(2)]
            self.m2 = [msg(l.at[t, f, full, w], rm.at[t, f, full, w], to[f]) for f in range(2)]

        def lead(self):
            for f in range(2):
                self.product(self.t, f)
                go(self.m1[f], False)

        def follow(self):
            for f in (1, 0):
                go(self.md[f], False)

        def start(self):
            self.lead()
            self.follow()

        def relay(self):
            t, w = self.t, self.w
            for f in range(2):
                self.m1[f].wait_send()
                self.m1[f].wait_recv()
                self.l[t, f, :, w] = (self.hold[t % 2, f, :, w] + self.rl[t, f, :, w].astype(F32)).astype(BF16)
                go(self.m2[f])

        def total(self, h):
            t, w = self.t, self.w
            return (self.acc[t, h, :, w] + self.rm[t, h, :, w].astype(F32) + self.rd[t, 1 - h, :, w].astype(F32))

        def finish(self):
            for f in range(2):
                self.md[f].wait_send()
                self.md[f].wait_recv()
            for f in range(2):
                self.m2[f].wait_recv()

    s2 = Sum(0, 128, zs, product2, acc2, hold2, l2, d2, rl2, rd2, rm2)
    s0 = [Sum(t, Q1 + t // 7 * 128, xs, product0, acc0, hold0, l0, d0, rl0, rd0, rm0) for t in range(8)]
    s1 = [Sum(t, Q2, ys, product1, acc1, hold1, l1, d1, rl1, rd1, rm1) for t in range(8)]

    def zmsgs(t, k, flip):
        w = (pl.ds(0, RC), s0[t].w)
        return [msg(d0.at[(t, 1 - f if flip else f) + w], rz.at[(k, t % 2, f) + w], zs[f]) for f in range(2)]

    zl = [zmsgs(t, 0, False) for t in (0, 1)]
    zm = [zmsgs(t, 1, False) for t in (2, 3)]
    zd = [zmsgs(t, 2, True) for t in (4, 5)]
    mp = [msg(d1.at[t], rp.at[t], pair) for t in range(4)]
    outs = []

    def put(src, dst):
        cp = pltpu.make_async_copy(src, dst, osem.at[len(outs)])
        cp.start()
        outs.append(cp)

    def cols(core_, o, n):
        return pl.ds(pl.multiple_of(core_ * HALF + o, 128), n)

    f0m, f1m = [], []

    def done0(t):
        s0[t].finish()
        p, s, w = t // 2, t % 2, s0[t].w
        for f in range(2):
            if p == 0:
                d0[t, f, :, w] = s0[t].total(f).astype(BF16)
                go(zl[s][f])
            elif p == 1:
                zl[s][f].wait_recv()
                d0[t, f, :, w] = (s0[t].total(f) + rz[0, s, f, :, w].astype(F32)).astype(BF16)
                go(zm[s][f])
            elif p == 2:
                d0[t, 1 - f, :, w] = s0[t].total(1 - f).astype(BF16)
                go(zd[s][f])
            else:
                zm[s][f].wait_recv()
                zd[s][f].wait_recv()
        if p == 3:
            for h in range(2):
                acc0[t, h, :, w] = s0[t].total(h)
                acc0[t, h, :, 0:Q1] += rz[1, s, h].astype(F32) + rz[2, s, 1 - h].astype(F32)
            f0m.append(go(msg(acc0.at[t, :, pl.ds(theirs, R), w], f0.at[s, :, :, w], core)))
            for h in range(2):
                put(acc0.at[t, h, pl.ds(mine, R), pl.ds(0, Q1)], gamma_ref.at[0, :, cols(c, h * Q + s * Q1, Q1)])
                if s == 1:
                    put(acc0.at[t, h, pl.ds(mine, R), pl.ds(Q1, 128)],
                        dens_ref.at[:, pl.ds(pl.multiple_of((c + h) * 128, 128), 128)])

    def land0(s):
        f0m[s].wait_recv()
        for h in range(2):
            put(f0.at[s, h, :, pl.ds(0, Q1)], gamma_ref.at[0, :, cols(1 - c, h * Q + s * Q1, Q1)])
        if s == 1:
            put(f0.at[s, 1 - c, :, pl.ds(Q1, 128)],
                dens_ref.at[:, pl.ds(pl.multiple_of((1 - c) * 256, 128), 128)])

    def done1(t):
        s1[t].finish()
        if t < 4:
            for h in range(2):
                d1[t, h] = s1[t].total(h).astype(BF16)
            go(mp[t])
            return
        s = t - 4
        mp[s].wait_recv()
        for h in range(2):
            acc1[t, h] = s1[t].total(h) + rp[s, h].astype(F32)
        for k in range(2):
            f1m.append(go(msg(acc1.at[t, :, pl.ds(pl.multiple_of(k * RC + theirs, 8), R)], f1.at[s, k], core)))
        for k in range(2):
            for h in range(2):
                put(acc1.at[t, h, pl.ds(pl.multiple_of(k * RC + mine, 8), R)],
                    gamma_ref.at[1 + k, :, cols(c, s * Q1 + h * Q2, Q2)])

    def land1(s):
        for k in range(2):
            f1m[s * 2 + k].wait_recv()
            for h in range(2):
                put(f1.at[s, k, h], gamma_ref.at[1 + k, :, cols(1 - c, s * Q1 + h * Q2, Q2)])

    s0[0].start()
    s1[0].start()
    s2.start()
    s0[0].relay()
    s0[1].start()
    s1[0].relay()
    s2.relay()
    s1[1].start()
    done0(0)
    done1(0)
    for t in range(1, 8):
        if t < 7:
            s0[t + 1].lead()
            s1[t + 1].lead()
        s0[t].relay()
        s1[t].relay()
        if t < 7:
            s0[t + 1].follow()
            s1[t + 1].follow()
        if t > 1:
            done0(t - 1)
            done1(t - 1)
        if t - 2 >= 4:
            land1(t - 6)
        if t == 3:
            s2.finish()
    land0(0)
    land1(2)
    done0(7)
    done1(7)
    land0(1)
    land1(3)
    for m in sent:
        m.wait_send()
    for cp in outs:
        cp.wait()


def write(gamma_in, dens_in, gamma_ref, dens_ref, gamma_via, dens_via, sem):
    spots = [(k, pl.ds(8 * r, 8), pl.ds(HALF * h, HALF)) for k in range(3) for r in range(3) for h in range(2)]
    parts = [(gamma_in.at[p], gamma_via.at[p], gamma_ref.at[p]) for p in spots] + [(dens_in, dens_via, dens_ref)]
    come = [pltpu.make_async_copy(p[0], p[1], sem.at[0, n]) for n, p in enumerate(parts)]
    leave = [pltpu.make_async_copy(p[1], p[2], sem.at[1, n]) for n, p in enumerate(parts)]
    for cp in come:
        cp.start()
    for cp, then in zip(come, leave):
        cp.wait()
        then.start()
    for cp in leave:
        cp.wait()


def shards(b_factors, occ_energy, vir_energy, pair_ids):
    vm = pl.BlockSpec(memory_space=pltpu.VMEM)
    V = pltpu.VMEM
    shapes = (jax.ShapeDtypeStruct((3, R, 2 * HALF), F32), jax.ShapeDtypeStruct((R, 16 * R), F32))
    anywhere = pl.BlockSpec(memory_space=pl.ANY)
    gamma, density = pl.pallas_call(
        kernel,
        out_shape=shapes,
        in_specs=[vm, vm, pl.BlockSpec(memory_space=pltpu.SMEM), anywhere],
        out_specs=(anywhere, anywhere),
        scratch_shapes=[
            V((3, R, 2 * HALF), BF16), V((ROWS, WID), BF16), V((ROWS, WID), BF16), V((3, RC, WID), F32), V((3, R, WID), F32),
            V((ROWS, ROWS), F32), V((ROWS, ROWS), F32),
            V((ROWS, ROWS), BF16), V((ROWS, ROWS), BF16), V((ROWS, ROWS), BF16),
            V((8, 2, RC, W0), F32), V((2, 2, RC, W0), F32), V((8, 2, RC, W0), BF16), V((8, 2, RC, W0), BF16),
            V((8, 2, RC, W0), BF16), V((8, 2, RC, W0), BF16), V((8, 2, RC, W0), BF16),
            V((8, 2, 2 * RC, Q2), F32), V((2, 2, 2 * RC, Q2), F32), V((8, 2, 2 * RC, Q2), BF16),
            V((8, 2, 2 * RC, Q2), BF16),
            V((8, 2, 2 * RC, Q2), BF16), V((8, 2, 2 * RC, Q2), BF16), V((8, 2, 2 * RC, Q2), BF16),
            V((1, 2, 4 * RC, 128), F32), V((1, 2, 4 * RC, 128), F32), V((1, 2, 4 * RC, 128), BF16),
            V((1, 2, 4 * RC, 128), BF16),
            V((1, 2, 4 * RC, 128), BF16), V((1, 2, 4 * RC, 128), BF16), V((1, 2, 4 * RC, 128), BF16),
            V((3, 2, 2, RC, Q1), BF16), V((4, 2, 2 * RC, Q2), BF16),
            V((2, 2, R, W0), F32), V((4, 2, 2, R, Q2), F32),
            pltpu.SemaphoreType.DMA((NMSG,)), pltpu.SemaphoreType.DMA((NMSG,)), pltpu.SemaphoreType.DMA((64,)),
        ],
        compiler_params=pltpu.CompilerParams(
            collective_id=0, has_side_effects=True, vmem_limit_bytes=61 * 2**20),
        cost_estimate=pl.CostEstimate(flops=15 * 10**9, bytes_accessed=4 * 10**6, transcendentals=0),
        name="mp2",
    )(vir_energy.reshape(1, R), occ_energy.reshape(12, 128), pair_ids, b_factors)
    return pl.pallas_call(
        write, out_shape=shapes, in_specs=[anywhere, anywhere], out_specs=(anywhere, anywhere),
        scratch_shapes=[V((3, R, 2 * HALF), F32), V((R, 16 * R), F32), pltpu.SemaphoreType.DMA((2, 19))], name="write",
    )(gamma, density)


def solution(mesh):
    in_specs = (P(None, ("row", "col"), None), P(), P(("row", "col")), P())
    out_specs = (P(None, ("row", "col"), None), P(("row", "col"), None))
    return jax.shard_map(shards, mesh=mesh, in_specs=in_specs, out_specs=out_specs, check_vma=False)
```

```python
import jax
import jax.numpy as jnp
from jax import lax
from jax.experimental import pallas as pl
from jax.experimental.pallas import tpu as pltpu
from jax.sharding import PartitionSpec as P

MESH = pl.DeviceIdType.MESH
F32, BF16 = jnp.float32, jnp.bfloat16
NT = (((1,), (1,)), ((), ()))

R = 24
RC = 2 * R
HALF = 4096
EXT = 128
WID = HALF + EXT
CUT = 2048
Q = 2048
W0 = Q // 2 + 128
ROWS = 16 * RC
NMSG = 224
Q1, Q2 = Q // 2, Q // 4
ORD = (0, 1, 3, 2)
POS = tuple(ORD.index(k) for k in range(4))
CHUNK = ((2, 2), (1, 3), (3, 1), (0, 0))


def kernel(vir_ref, occ_ref, pid_ref, b_hbm, gamma_ref, dens_ref,
           b_ref, A, B, st, snd, ip, ir, amp, ampt, ampd,
           acc0, hold0, l0, d0, rl0, rd0, rm0,
           acc1, hold1, l1, d1, rl1, rd1, rm1,
           acc2, hold2, l2, d2, rl2, rd2, rm2,
           rz, rp, f0, f1, ssem, rsem, osem):
    row, col = lax.axis_index("row"), lax.axis_index("col")
    x, y, z, c = col // 4, row % 4, (col // 2) % 2 * 4 + row // 4, col % 2

    def dev(x, y, z, c):
        return (z % 4 * 4 + y, x * 4 + z // 4 * 2 + c)

    xs = [dev((x + 1) % 4, y, z, c), dev((x + 3) % 4, y, z, c)]
    ys = [dev(x, (y + 1) % 4, z, c), dev(x, (y + 3) % 4, z, c)]
    zs = [dev(x, y, (z + 2) % 8, c), dev(x, y, (z + 6) % 8, c)]
    far = dev(x, y, (z + 4) % 8, c)
    pair = dev(x, y, z + 1 - 2 * (z % 2), c)
    core = dev(x, y, z, 1 - c)
    peers = xs + ys + zs + [far, pair, core]

    barrier = pltpu.get_barrier_semaphore()
    for p in peers:
        pl.semaphore_signal(barrier, inc=1, device_id=p, device_id_type=MESH)

    load = pltpu.make_async_copy(b_hbm, b_ref, osem.at[63])
    load.start()

    count = [0]

    def msg(src, dst, to):
        i = count[0]
        count[0] += 1
        return pltpu.make_async_remote_copy(
            src_ref=src, dst_ref=dst, send_sem=ssem.at[i], recv_sem=rsem.at[i],
            device_id=to, device_id_type=MESH)

    sent = []

    def go(m, later=True):
        m.start()
        if later:
            sent.append(m)
        return m

    lane = lax.broadcasted_iota(jnp.int32, (R, EXT), 1)
    e = vir_ref[...]
    diag = lax.broadcasted_iota(jnp.int32, (R, R), 0) == lax.broadcasted_iota(jnp.int32, (R, R), 1)
    e_hi = jnp.sum(jnp.where(diag, (e >> 6).astype(F32), 0.0), axis=1, keepdims=True) * (64.0 / 1024.0)
    e_lo = jnp.sum(jnp.where(diag, (e & 63).astype(F32), 0.0), axis=1, keepdims=True) * (1.0 / 1024.0)
    occ = occ_ref[...]
    place = lax.broadcasted_iota(jnp.int32, occ.shape, 0) * occ.shape[1] + lax.broadcasted_iota(
        jnp.int32, occ.shape, 1)

    def level(k):
        picked = jnp.where(place == pid_ref[k], occ.astype(F32), 0.0)
        return jnp.sum(jnp.sum(picked, axis=1, keepdims=True), axis=0, keepdims=True)

    zero = jnp.zeros((R, EXT), F32)
    exts = [jnp.where(lane == 0, e_hi, jnp.where(lane == 1, e_lo, jnp.where(
        lane < 4, 1.0, jnp.where(lane < 6, -1.0, zero))))]
    for k in range(2):
        s = level(0) + level(1 + k)
        s_hi = jnp.floor(s * (1.0 / 64.0))
        s_lo = s - s_hi * 64.0
        exts.append(jnp.where(lane < 2, 1.0, jnp.where(lane == 2, e_hi, jnp.where(lane == 3, e_lo, jnp.where(
            lane == 4, s_hi * (64.0 / 1024.0), jnp.where(lane == 5, s_lo * (1.0 / 1024.0), zero))))))

    mine = pl.multiple_of(c * R, 8)
    theirs = pl.multiple_of((1 - c) * R, 8)

    load.wait()

    @pl.loop(0, 3)
    def _(m):
        @pl.loop(0, HALF // 512)
        def _(n):
            o = pl.multiple_of(n * 512, 128)
            st[m, pl.ds(mine, R), pl.ds(o, 512)] = b_ref[m, :, pl.ds(pl.multiple_of(c * HALF + o, 128), 512)].astype(F32)
            snd[m, :, pl.ds(o, 512)] = b_ref[m, :, pl.ds(pl.multiple_of((1 - c) * HALF + o, 128), 512)].astype(F32)

    for m in range(3):
        st[m, pl.ds(mine, R), HALF:] = exts[m]
        snd[m, :, HALF:] = exts[m]

    pl.semaphore_wait(barrier, len(peers))
    swap = [go(msg(snd.at[m], st.at[m, pl.ds(mine, R)], core)) for m in range(3)]

    def arow(i, j):
        return (POS[i] * 4 + POS[j]) * RC

    def brow(b, j):
        return (b * 4 + POS[j]) * 2 * RC

    H = [pl.ds(0, CUT), pl.ds(CUT, WID - CUT)]
    H4 = [pl.ds(0, 1024), pl.ds(1024, 1024), pl.ds(2048, 1024), pl.ds(3072, WID - 3072)]

    class Ring:
        def __init__(self, buf, at, n, to, cut):
            rows = lambda s: pl.ds(at[s], n)
            self.own = [[msg(buf.at[rows(0), cut[h]], buf.at[rows((3, 1)[d]), cut[h]], to[d]) for h in range(2)]
                        for d in range(2)]
            self.fwd = [msg(buf.at[rows((3, 1)[d]), cut[d]], buf.at[rows(2), cut[d]], to[d]) for d in range(2)]

        def first(self):
            for d in range(2):
                go(self.own[d][d])

        def second(self):
            for d in range(2):
                go(self.own[d][1 - d])

        def forward(self, ds=(0, 1)):
            for d in ds:
                self.own[d][d].wait_recv()
                go(self.fwd[d])

        def rest(self):
            for d in range(2):
                self.own[d][1 - d].wait_recv()

        def finish(self):
            for d in range(2):
                self.fwd[d].wait_recv()

    zown = [[msg(A.at[pl.ds(0, RC), H[h]], A.at[pl.ds(arow((3, 1)[d], 0), RC), H[h]], zs[d]) for h in range(2)]
            for d in range(2)]
    zfar = [[msg(A.at[pl.ds(arow((3, 1)[d], 0), RC), H4[2 * d + p]], A.at[pl.ds(arow(2, 0), RC), H4[2 * d + p]], zs[d])
             for p in range(2)] for d in range(2)]
    xr = [Ring(A, [arow(i, j) for j in range(4)], RC, xs, H) for i in (0, 1, 3)]
    x0, x1, x3 = xr
    x2 = [Ring(A, [arow(2, j) for j in range(4)], RC, xs, [H4[p], H4[2 + p]]) for p in range(2)]
    y0 = Ring(B, [brow(0, j) for j in range(4)], 2 * RC, ys, H)
    y1 = [Ring(B, [brow(1, j) for j in range(4)], 2 * RC, ys, [H4[p], H4[2 + p]]) for p in range(2)]
    pr = [[msg(B.at[pl.ds(0, 2 * RC), H4[p + q]], B.at[pl.ds(brow(1, 0), 2 * RC), H4[p + q]], pair) for q in (0, 2)]
          for p in range(2)]

    def integral(r, n, o0, o1, w):
        @pl.loop(0, (o1 - o0) // w)
        def _(k):
            o = pl.ds(pl.multiple_of(o0 + k * w, 128), w)
            ip[r:r + n, o] = lax.dot_general(A[r:r + n, 0:HALF], B[o, 0:HALF], NT, preferred_element_type=F32)

    def swapped(r, n, o0, o1):
        part = (pl.ds(r, n), pl.ds(o0, o1 - o0))
        return go(msg(ip.at[part], ir.at[part], core))

    def slot(s):
        i, j = ORD[s // 4], ORD[s % 4]
        return i % 2 * (ROWS // 2) + ((x + j) % 4 * 2 + (z + 2 * i) % 8 // 4) * RC

    def amplitude(r, n, o0, o1):
        @pl.loop(0, (o1 - o0) // 128)
        def _(k):
            o = pl.ds(pl.multiple_of(o0 + k * 128, 128), 128)
            rows = pl.ds(r, n)
            den = lax.dot_general(A[rows, HALF:], B[o, HALF:], NT, preferred_element_type=F32)
            t = ((ip[rows, o] + ir[rows, o]) / (0.0 - den)).astype(BF16)
            amp[rows, o] = t
            ampt[o, rows] = t.astype(F32).T.astype(BF16)
            for s in range(16):
                lo, hi = max(r, s * RC), min(r + n, s * RC + RC)
                if lo < hi:
                    ampd[pl.ds(pl.multiple_of(slot(s) + lo - s * RC, 16), hi - lo), o] = t[lo - r:hi - r]

    def settle(buf, to, m):
        swap[m].wait_recv()

        @pl.loop(0, 3)
        def _(n):
            o = pl.ds(pl.multiple_of(n * 1408, 128), 1408)
            buf[to:to + RC, o] = st[m, :, o].astype(BF16)

    settle(A, 0, 0)
    for d in range(2):
        go(zown[d][d])
    x0.first()
    for d in range(2):
        go(zown[d][1 - d])
    x0.second()
    for k in range(2):
        settle(B, k * RC, 1 + k)
    y0.first()
    y0.second()
    x0.forward()
    for d in range(2):
        zown[d][d].wait_recv()
    for q in range(2):
        go(pr[0][q])
    go(x3.own[0][0])
    go(x1.own[1][1])
    go(x3.own[1][0])
    go(x1.own[0][1])
    y0.forward()
    for d in range(2):
        zown[d][1 - d].wait_recv()
    for q in range(2):
        go(pr[1][q])
    go(x3.own[0][1])
    go(x1.own[1][0])
    go(x3.own[1][1])
    go(x1.own[0][0])
    x3.forward((0,))
    x1.forward((1,))
    for q in range(2):
        pr[0][q].wait_recv()
    y1[0].first()
    y1[0].second()
    for d in range(2):
        go(zfar[d][0])
    for r in (x0, y0):
        r.rest()
        r.finish()
    integral(0, 192, 0, 384, 128)
    x3.forward((1,))
    x1.forward((0,))
    for q in range(2):
        pr[1][q].wait_recv()
    y1[1].first()
    y1[1].second()
    for d in range(2):
        go(zfar[d][1])
    for d in range(2):
        zfar[d][0].wait_recv()
    x2[0].first()
    x2[0].second()
    y1[0].forward()
    for d in range(2):
        zfar[d][1].wait_recv()
    x2[1].first()
    x2[1].second()
    x2[0].forward()
    for r in (x1, x3):
        r.rest()
        r.finish()
    integral(192, 320, 0, 384, 128)
    y1[1].forward()
    x2[1].forward()
    for r in y1:
        r.rest()
    integral(0, 512, 384, 512, 128)
    early = swapped(0, 512, 0, 512)
    x2[0].rest()
    x2[0].finish()
    y1[0].finish()
    early.wait_recv()
    amplitude(0, 512, 0, 512)
    x2[1].rest()
    x2[1].finish()
    y1[1].finish()
    integral(512, 256, 0, 512, 256)
    late = [swapped(512, 256, 0, 512)]
    integral(0, ROWS, 512, ROWS, 256)
    late.append(swapped(0, ROWS, 512, ROWS))
    late[0].wait_recv()
    amplitude(512, 256, 0, 512)
    late[1].wait_recv()
    amplitude(0, ROWS, 512, ROWS)

    def store(t, h, n, cs, out, acc, hold, l, d):
        acc[t, h, :, cs] = out[0:n]
        l[t, h, :, cs] = out[3 * n:4 * n].astype(BF16)
        if h == 0:
            hold[t % 2, 0, :, cs] = out[n:2 * n]
            d[t, 1, :, cs] = out[2 * n:3 * n].astype(BF16)
        else:
            hold[t % 2, 1, :, cs] = out[2 * n:3 * n]
            d[t, 0, :, cs] = out[n:2 * n].astype(BF16)

    def product0(t, h):
        i, s = CHUNK[t // 2][h], t % 2
        lhs = amp[POS[i] * 4 * RC:(POS[i] + 1) * 4 * RC, :]

        @pl.loop(0, Q1 // 512)
        def _(n):
            o = pl.multiple_of(n * 512, 512)
            out = jnp.dot(lhs, B[:, pl.ds(o + h * Q + s * Q1, 512)], preferred_element_type=F32)
            store(t, h, RC, pl.ds(o, 512), out, acc0, hold0, l0, d0)

        if t == 7:
            store(t, h, RC, pl.ds(Q1, 128), s2.total(h), acc0, hold0, l0, d0)

    def product1(t, h):
        b, s = 1 - t // 4, t % 4
        lhs = ampt[b * ROWS // 2:(b + 1) * ROWS // 2, :]

        @pl.loop(0, Q2 // 256)
        def _(n):
            o = pl.multiple_of(n * 256, 256)
            out = jnp.dot(lhs, A[:, pl.ds(o + s * Q1 + h * Q2, 256)], preferred_element_type=F32)
            store(t, h, 2 * RC, pl.ds(o, 256), out, acc1, hold1, l1, d1)

    def product2(t, h):
        n = 4 * RC
        for i in range(4):
            rhs = ampd[pl.ds(pl.multiple_of(i % 2 * (ROWS // 2) + h * 128 + c * 128, 128), 128), :]
            out = lax.dot_general(amp[POS[i] * n:(POS[i] + 1) * n, :], rhs, NT, preferred_element_type=F32)
            if i == 0:
                acc2[t, h] = out
            elif i == 2:
                l2[t, h] = out.astype(BF16)
            elif i == 1 + 2 * h:
                hold2[t, h] = out
            else:
                d2[t, 1 - h] = out.astype(BF16)

    class Sum:
        def __init__(self, t, width, to, product, acc, hold, l, d, rl, rd, rm):
            w = pl.ds(0, width)
            full = pl.ds(0, acc.shape[2])
            self.t, self.w, self.product = t, w, product
            self.acc, self.hold, self.l, self.rd, self.rl, self.rm = acc, hold, l, rd, rl, rm
            self.m1 = [msg(l.at[t, f, full, w], rl.at[t, f, full, w], to[f]) for f in range(2)]
            self.md = [msg(d.at[t, f, full, w], rd.at[t, f, full, w], to[f]) for f in range(2)]
            self.m2 = [msg(l.at[t, f, full, w], rm.at[t, f, full, w], to[f]) for f in range(2)]

        def lead(self):
            for f in range(2):
                self.product(self.t, f)
                go(self.m1[f], False)

        def follow(self):
            for f in (1, 0):
                go(self.md[f], False)

        def start(self):
            self.lead()
            self.follow()

        def relay(self):
            t, w = self.t, self.w
            for f in range(2):
                self.m1[f].wait_send()
                self.m1[f].wait_recv()
                self.l[t, f, :, w] = (self.hold[t % 2, f, :, w] + self.rl[t, f, :, w].astype(F32)).astype(BF16)
                go(self.m2[f])

        def total(self, h):
            t, w = self.t, self.w
            return (self.acc[t, h, :, w] + self.rm[t, h, :, w].astype(F32) + self.rd[t, 1 - h, :, w].astype(F32))

        def finish(self):
            for f in range(2):
                self.md[f].wait_send()
                self.md[f].wait_recv()
            for f in range(2):
                self.m2[f].wait_recv()

    s2 = Sum(0, 128, zs, product2, acc2, hold2, l2, d2, rl2, rd2, rm2)
    s0 = [Sum(t, Q1 + t // 7 * 128, xs, product0, acc0, hold0, l0, d0, rl0, rd0, rm0) for t in range(8)]
    s1 = [Sum(t, Q2, ys, product1, acc1, hold1, l1, d1, rl1, rd1, rm1) for t in range(8)]

    def zmsgs(t, k, flip):
        w = (pl.ds(0, RC), s0[t].w)
        return [msg(d0.at[(t, 1 - f if flip else f) + w], rz.at[(k, t % 2, f) + w], zs[f]) for f in range(2)]

    zl = [zmsgs(t, 0, False) for t in (0, 1)]
    zm = [zmsgs(t, 1, False) for t in (2, 3)]
    zd = [zmsgs(t, 2, True) for t in (4, 5)]
    mp = [msg(d1.at[t], rp.at[t], pair) for t in range(4)]
    outs = []

    def put(src, dst):
        cp = pltpu.make_async_copy(src, dst, osem.at[len(outs)])
        cp.start()
        outs.append(cp)

    def cols(core_, o, n):
        return pl.ds(pl.multiple_of(core_ * HALF + o, 128), n)

    f0m, f1m = [], []

    def done0(t):
        s0[t].finish()
        p, s, w = t // 2, t % 2, s0[t].w
        for f in range(2):
            if p == 0:
                d0[t, f, :, w] = s0[t].total(f).astype(BF16)
                go(zl[s][f])
            elif p == 1:
                zl[s][f].wait_recv()
                d0[t, f, :, w] = (s0[t].total(f) + rz[0, s, f, :, w].astype(F32)).astype(BF16)
                go(zm[s][f])
            elif p == 2:
                d0[t, 1 - f, :, w] = s0[t].total(1 - f).astype(BF16)
                go(zd[s][f])
            else:
                zm[s][f].wait_recv()
                zd[s][f].wait_recv()
        if p == 3:
            for h in range(2):
                acc0[t, h, :, w] = s0[t].total(h)
                acc0[t, h, :, 0:Q1] += rz[1, s, h].astype(F32) + rz[2, s, 1 - h].astype(F32)
            f0m.append(go(msg(acc0.at[t, :, pl.ds(theirs, R), w], f0.at[s, :, :, w], core)))
            for h in range(2):
                put(acc0.at[t, h, pl.ds(mine, R), pl.ds(0, Q1)], gamma_ref.at[0, :, cols(c, h * Q + s * Q1, Q1)])
                if s == 1:
                    put(acc0.at[t, h, pl.ds(mine, R), pl.ds(Q1, 128)],
                        dens_ref.at[:, pl.ds(pl.multiple_of((c + h) * 128, 128), 128)])

    def land0(s):
        f0m[s].wait_recv()
        for h in range(2):
            put(f0.at[s, h, :, pl.ds(0, Q1)], gamma_ref.at[0, :, cols(1 - c, h * Q + s * Q1, Q1)])
        if s == 1:
            put(f0.at[s, 1 - c, :, pl.ds(Q1, 128)],
                dens_ref.at[:, pl.ds(pl.multiple_of((1 - c) * 256, 128), 128)])

    def done1(t):
        s1[t].finish()
        if t < 4:
            for h in range(2):
                d1[t, h] = s1[t].total(h).astype(BF16)
            go(mp[t])
            return
        s = t - 4
        mp[s].wait_recv()
        for h in range(2):
            acc1[t, h] = s1[t].total(h) + rp[s, h].astype(F32)
        for k in range(2):
            f1m.append(go(msg(acc1.at[t, :, pl.ds(pl.multiple_of(k * RC + theirs, 8), R)], f1.at[s, k], core)))
        for k in range(2):
            for h in range(2):
                put(acc1.at[t, h, pl.ds(pl.multiple_of(k * RC + mine, 8), R)],
                    gamma_ref.at[1 + k, :, cols(c, s * Q1 + h * Q2, Q2)])

    def land1(s):
        for k in range(2):
            f1m[s * 2 + k].wait_recv()
            for h in range(2):
                put(f1.at[s, k, h], gamma_ref.at[1 + k, :, cols(1 - c, s * Q1 + h * Q2, Q2)])

    s0[0].start()
    s1[0].start()
    s2.start()
    s0[0].relay()
    s0[1].start()
    s1[0].relay()
    s2.relay()
    s1[1].start()
    done0(0)
    done1(0)
    for t in range(1, 8):
        if t < 7:
            s0[t + 1].lead()
            s1[t + 1].lead()
        s0[t].relay()
        s1[t].relay()
        if t < 7:
            s0[t + 1].follow()
            s1[t + 1].follow()
        if t > 1:
            done0(t - 1)
            done1(t - 1)
        if t - 2 >= 4:
            land1(t - 6)
        if t == 3:
            s2.finish()
    land0(0)
    land1(2)
    done0(7)
    done1(7)
    land0(1)
    land1(3)
    for m in sent:
        m.wait_send()
    for cp in outs:
        cp.wait()


def write(gamma_in, dens_in, gamma_ref, dens_ref, gamma_via, dens_via, sem):
    parts = [(gamma_in.at[k, pl.ds(8 * r, 8)], gamma_via.at[k, pl.ds(8 * r, 8)], gamma_ref.at[k, pl.ds(8 * r, 8)])
             for k in range(3) for r in range(3)] + [(dens_in, dens_via, dens_ref)]
    come = [pltpu.make_async_copy(p[0], p[1], sem.at[0, n]) for n, p in enumerate(parts)]
    leave = [pltpu.make_async_copy(p[1], p[2], sem.at[1, n]) for n, p in enumerate(parts)]
    for cp in come:
        cp.start()
    for cp, then in zip(come, leave):
        cp.wait()
        then.start()
    for cp in leave:
        cp.wait()


def shards(b_factors, occ_energy, vir_energy, pair_ids):
    vm = pl.BlockSpec(memory_space=pltpu.VMEM)
    V = pltpu.VMEM
    shapes = (jax.ShapeDtypeStruct((3, R, 2 * HALF), F32), jax.ShapeDtypeStruct((R, 16 * R), F32))
    anywhere = pl.BlockSpec(memory_space=pl.ANY)
    gamma, density = pl.pallas_call(
        kernel,
        out_shape=shapes,
        in_specs=[vm, vm, pl.BlockSpec(memory_space=pltpu.SMEM), anywhere],
        out_specs=(anywhere, anywhere),
        scratch_shapes=[
            V((3, R, 2 * HALF), BF16), V((ROWS, WID), BF16), V((ROWS, WID), BF16), V((3, RC, WID), F32), V((3, R, WID), F32),
            V((ROWS, ROWS), F32), V((ROWS, ROWS), F32),
            V((ROWS, ROWS), BF16), V((ROWS, ROWS), BF16), V((ROWS, ROWS), BF16),
            V((8, 2, RC, W0), F32), V((2, 2, RC, W0), F32), V((8, 2, RC, W0), BF16), V((8, 2, RC, W0), BF16),
            V((8, 2, RC, W0), BF16), V((8, 2, RC, W0), BF16), V((8, 2, RC, W0), BF16),
            V((8, 2, 2 * RC, Q2), F32), V((2, 2, 2 * RC, Q2), F32), V((8, 2, 2 * RC, Q2), BF16),
            V((8, 2, 2 * RC, Q2), BF16),
            V((8, 2, 2 * RC, Q2), BF16), V((8, 2, 2 * RC, Q2), BF16), V((8, 2, 2 * RC, Q2), BF16),
            V((1, 2, 4 * RC, 128), F32), V((1, 2, 4 * RC, 128), F32), V((1, 2, 4 * RC, 128), BF16),
            V((1, 2, 4 * RC, 128), BF16),
            V((1, 2, 4 * RC, 128), BF16), V((1, 2, 4 * RC, 128), BF16), V((1, 2, 4 * RC, 128), BF16),
            V((3, 2, 2, RC, Q1), BF16), V((4, 2, 2 * RC, Q2), BF16),
            V((2, 2, R, W0), F32), V((4, 2, 2, R, Q2), F32),
            pltpu.SemaphoreType.DMA((NMSG,)), pltpu.SemaphoreType.DMA((NMSG,)), pltpu.SemaphoreType.DMA((64,)),
        ],
        compiler_params=pltpu.CompilerParams(
            collective_id=0, has_side_effects=True, vmem_limit_bytes=61 * 2**20),
        cost_estimate=pl.CostEstimate(flops=15 * 10**9, bytes_accessed=4 * 10**6, transcendentals=0),
        name="mp2",
    )(vir_energy.reshape(1, R), occ_energy.reshape(12, 128), pair_ids, b_factors)
    return pl.pallas_call(
        write, out_shape=shapes, in_specs=[anywhere, anywhere], out_specs=(anywhere, anywhere),
        scratch_shapes=[V((3, R, 2 * HALF), F32), V((R, 16 * R), F32), pltpu.SemaphoreType.DMA((2, 10))], name="write",
    )(gamma, density)


def solution(mesh):
    in_specs = (P(None, ("row", "col"), None), P(), P(("row", "col")), P())
    out_specs = (P(None, ("row", "col"), None), P(("row", "col"), None))
    return jax.shard_map(shards, mesh=mesh, in_specs=in_specs, out_specs=out_specs, check_vma=False)
```
